32 devices in a mesh: grp: 2 (over x), gz: 16 (over z, y, core).
Axes of the slice: x: 2, y: 2, z: 4, core: 2. Of those that a mesh axis runs over, the one named last changes fastest.
Arguments:
- vectors: bfloat16 [4, 384, 3, 16, 768], P('grp', None, None, 'gz'), parts along dimension 0, may hold values from -6 to 6
- links: float32 [4, 2, 3, 3, 16, 768], P('grp', None, None, None, 'gz'), parts along dimension 0, may hold values from -6 to 6
Outputs:
- elementals: float32 [384, 8, 384], P('gz', 'grp'), parts along dimension 1
The draws below stay inside these ranges and needn't reach their ends.
There are 2 independent parts, one for each index of `grp`. The reference program is written for one: setup_inputs(seed, part) draws one part's arguments, and reference() takes and returns one part's arrays. A program takes and returns all parts, laid end to end along the dimension named above; each array names one. Nothing has to cross between parts.
All inputs are finite; a program needn't handle non-finite values.
Results may differ from the reference program's by a relative error of at most 0.008.
Values may be sent and summed in bfloat16 or wider, within the bound.
No kernel may reach another device: no remote copies, remote signals or barrier semaphores. Data moves between devices by JAX's collectives and lax.ppermute only.
A program may use at most 64 MiB of HBM per device.

```python
import math
import jax
import jax.numpy as jnp
from jax import lax

V = 384
X = 64
YW = 12
NZ = 16


def steps_of(key, shape, cuts, smallest, high):
    level = 1.0
    for dim, blocks in cuts:
        heights = jax.random.uniform(jax.random.fold_in(jax.random.fold_in(key, 6), dim), (blocks,), jnp.float32, smallest / len(cuts), high / len(cuts))
        level = level * jnp.repeat(jnp.exp(heights), shape[dim] // blocks).reshape((-1,) + (1,) * (len(shape) - 1 - dim))
    return level


def noise(own_key, dims, scale, most, shards=(), dtype=jnp.bfloat16):
    values = jax.random.normal(own_key, dims, jnp.float32) * scale
    if len(shards) > 0:
        values = steps_of(own_key, dims, shards, -0.22, 0.18) * values
    return jnp.clip(values, min=-most, max=most).astype(dtype)


def setup_inputs(seed: int = 0, part: int = 0) -> dict:
    key_of = jax.random.split(jax.random.key(seed), 3)
    part_keys = jax.random.split(jax.random.fold_in(key_of[2], part), 3)
    vectors = noise(part_keys[0], (2, V, 3, NZ, YW * X), 1.0, 6.0, ((3, 16),))
    links = noise(part_keys[1], (2, 2, 3, 3, NZ, YW * X), 0.41, 6.0, ((4, 16),), jnp.float32)
    return {"vectors": vectors, "links": links}


def forward_hop(links_part, field):

    def contract(first, second):
        return jnp.einsum('ab...,vb...->va...', first, second)
    real_part = contract(links_part[0], field[0]) - contract(links_part[1], field[1])
    imag_part = contract(links_part[0], field[1]) + contract(links_part[1], field[0])
    return jnp.stack([real_part, imag_part], axis=0)

def roll_sites(array, amount, width):
    shape = array.shape
    reshaped = array.reshape(shape[:-1] + (shape[-1] // width, width))
    return jnp.roll(reshaped, amount, axis=-1).reshape(shape)

def elemental_block(left, right):
    rows = left.shape[1]
    cols = right.shape[1]
    left_flat = left.reshape(2, rows, -1)
    right_flat = right.reshape(2, cols, -1)

    def inner(first, second):
        return lax.dot_general(first, second, (((1,), (1,)), ((), ())), preferred_element_type=jnp.float32)
    real_part = inner(left_flat[0], right_flat[0]) + inner(left_flat[1], right_flat[1])
    imag_part = inner(left_flat[0], right_flat[1]) - inner(left_flat[1], right_flat[0])
    return jnp.stack([real_part, imag_part], axis=1)

def reference(vectors, links):
    planes = vectors.shape[3]
    count = vectors.shape[1]

    def step(index, accum):
        here = jnp.asarray(index).astype(jnp.int32)
        after = ((here + 1) % planes).astype(jnp.int32)
        plane_here = lax.dynamic_index_in_dim(vectors, here, 3, keepdims=False)
        plane_after = lax.dynamic_index_in_dim(vectors, after, 3, keepdims=False).astype(jnp.float32)
        links_here = lax.dynamic_index_in_dim(links, here, 4, keepdims=False)
        here_float = plane_here.astype(jnp.float32)
        disp_x = forward_hop(links_here[:, 0], roll_sites(here_float, -1, X)).astype(jnp.bfloat16)
        disp_z = forward_hop(links_here[:, 1], plane_after).astype(jnp.bfloat16)
        term = jnp.concatenate([elemental_block(plane_here, disp_x), elemental_block(plane_here, disp_z)], axis=1)
        return accum + term
    start = jnp.zeros((count, 4, count), jnp.float32)
    total = lax.fori_loop(0, planes, step, start)
    flipped = jnp.transpose(total, (2, 1, 0))
    signs = jnp.array([1.0, -1.0, 1.0, -1.0], jnp.float32).reshape(1, 4, 1)
    return (total - signs * flipped) * (1.0 / math.sqrt(12.0 * X * YW * NZ))
```

```python
import functools
import math

import jax
import jax.numpy as jnp
from jax import lax
from jax.experimental import pallas as pl
from jax.experimental.pallas import tpu as pltpu
from jax.sharding import PartitionSpec as P

X = 64
LANES = 128
ROWS = 16


def passed_along(block, axis, distance):
    devices = range(lax.axis_size(axis))
    route = [((i - distance) % len(devices), i) for i in devices]
    return lax.ppermute(block, axis, route)


def displace(field_ref, u_ref, d_ref, roll):
    count, sites = field_ref.shape[1:]
    for t in range(sites // LANES):
        lanes = slice(t * LANES, (t + 1) * LANES)

        def link(part, a, b):
            row = (part * 3 + a) * 3 + b
            return jnp.broadcast_to(u_ref[row : row + 1, lanes], (ROWS, LANES))

        u = [[[link(p, a, b) for b in range(3)] for a in range(3)] for p in range(2)]
        if roll:
            lane = lax.broadcasted_iota(jnp.int32, (ROWS, LANES), 1)
            last = (lane & (X - 1)) == X - 1

        def body(m, carry):
            rows = pl.ds(pl.multiple_of(m * ROWS, ROWS), ROWS)
            v = []
            for k in range(6):
                value = field_ref[k, rows, lanes].astype(jnp.float32)
                if roll:
                    ahead = pltpu.roll(value, LANES - 1, 1)
                    around = pltpu.roll(value, X - 1, 1)
                    value = jnp.where(last, around, ahead)
                v.append(value)
            re, im = v[:3], v[3:]
            for a in range(3):
                ur, ui = u[0][a], u[1][a]
                dr = ur[0] * re[0] - ui[0] * im[0]
                di = ur[0] * im[0] + ui[0] * re[0]
                for b in (1, 2):
                    dr = dr + (ur[b] * re[b] - ui[b] * im[b])
                    di = di + (ur[b] * im[b] + ui[b] * re[b])
                d_ref[a, rows, lanes] = dr.astype(jnp.bfloat16)
                rows_i = pl.ds(pl.multiple_of(count + m * ROWS, ROWS), ROWS)
                d_ref[a, rows_i, lanes] = di.astype(jnp.bfloat16)
            return carry

        lax.fori_loop(0, count // ROWS, body, 0, unroll=2)


def kernel(roll, own, left_ref, *refs):
    if roll:
        u_ref, out_ref, d_ref = refs
        field_ref = left_ref
    else:
        field_ref, u_ref, out_ref, d_ref = refs
    count = left_ref.shape[1]
    displace(field_ref, u_ref, d_ref, roll)

    def inner(part):
        total = None
        for a in range(3):
            term = lax.dot_general(
                left_ref[part * 3 + a], d_ref[a], (((1,), (1,)), ((), ())),
                preferred_element_type=jnp.float32,
            )
            total = term if total is None else total + term
        return total

    from_re, from_im = inner(0), inner(1)
    sum_re = from_re[:, :count] + from_im[:, count:]
    sum_im = from_re[:, count:] - from_im[:, :count]
    re = sum_re - sum_re.T
    im = sum_im + sum_im.T
    if own % 8 == 0:
        for g in range(count // own):
            rows = slice(g * own, (g + 1) * own)
            both = jnp.concatenate([re[rows], im[rows]], axis=0)
            out_ref[g] = both.astype(jnp.bfloat16)
    else:
        out_ref[0] = re.astype(jnp.bfloat16)
        out_ref[1] = im.astype(jnp.bfloat16)


def direction(left, field, u, slabs):
    count, sites = left.shape[1:]
    own = count // slabs
    roll = field is None
    blocks = (slabs, 2 * own, count) if own % 8 == 0 else (2, count, count)
    operands = (left, u) if roll else (left, field, u)
    out = pl.pallas_call(
        functools.partial(kernel, roll, own),
        out_shape=jax.ShapeDtypeStruct(blocks, jnp.bfloat16),
        in_specs=[pl.BlockSpec(memory_space=pltpu.VMEM)] * len(operands),
        out_specs=pl.BlockSpec(memory_space=pltpu.VMEM),
        scratch_shapes=[pltpu.VMEM((3, 2 * count, sites), jnp.bfloat16)],
        compiler_params=pltpu.CompilerParams(vmem_limit_bytes=40 * 2**20),
        cost_estimate=pl.CostEstimate(
            flops=8 * count * count * 3 * sites,
            bytes_accessed=4 * 6 * count * sites,
            transcendentals=0,
        ),
    )(*operands)
    if own % 8 != 0:
        out = out.reshape(2, slabs, own, count).transpose(1, 0, 2, 3).reshape(slabs, 2 * own, count)
    return out


def shards(vectors, links):
    slabs = lax.axis_size("gz")
    count, planes, sites = vectors.shape[1], vectors.shape[3], vectors.shape[4]
    assert planes == 1
    own = count // slabs
    scale = 1.0 / math.sqrt(12.0 * sites * planes * slabs)
    field = jnp.transpose(vectors, (0, 2, 3, 1, 4)).reshape(6, count, sites)
    face = passed_along(field, "gz", -1)
    links_x = links[:, 0].reshape(18, sites)
    links_z = links[:, 1].reshape(18, sites)
    term_x = direction(field, None, links_x, slabs)
    got_x = lax.all_to_all(term_x, "gz", 0, 0)
    term_z = direction(field, face, links_z, slabs)
    got_z = lax.all_to_all(term_z, "gz", 0, 0)

    def total(got):
        return jnp.sum(got.astype(jnp.float32), axis=0).reshape(2, own, count)

    both = jnp.concatenate([total(got_x), total(got_z)], axis=0)
    return jnp.transpose(both, (1, 0, 2)) * scale


def solution(mesh):
    return jax.shard_map(
        shards,
        mesh=mesh,
        in_specs=(P("grp", None, None, "gz", None), P("grp", None, None, None, "gz", None)),
        out_specs=P("gz", "grp", None),
        check_vma=False,
    )
```

```python
import functools
import math

import jax
import jax.numpy as jnp
from jax import lax
from jax.experimental import pallas as pl
from jax.experimental.pallas import tpu as pltpu
from jax.sharding import PartitionSpec as P

X = 64
LANES = 128
ROWS = 16
CHUNKS = 3


def passed_along(block, axis, distance):
    devices = range(lax.axis_size(axis))
    route = [((i - distance) % len(devices), i) for i in devices]
    return lax.ppermute(block, axis, route)


def swapped(block, axis):
    return lax.ppermute(block, axis, [(i, i ^ 1) for i in range(lax.axis_size(axis))])


def displace(field_ref, u_ref, d_ref, roll):
    sites = field_ref.shape[2]
    count = d_ref.shape[0] // 2
    half = ROWS // 2
    for t in range(sites // LANES):
        lanes = slice(t * LANES, (t + 1) * LANES)

        def link(part, a, b):
            row = (part * 3 + a) * 3 + b
            return jnp.broadcast_to(u_ref[row : row + 1, lanes], (half, LANES))

        u = [[[link(p, a, b) for b in range(3)] for a in range(3)] for p in range(2)]
        if roll:
            lane = lax.broadcasted_iota(jnp.int32, (ROWS, LANES), 1)
            last = (lane & (X - 1)) == X - 1

        def body(m, carry):
            rows = pl.ds(pl.multiple_of(m * ROWS, ROWS), ROWS)
            v = []
            for k in range(6):
                value = field_ref[k, rows, lanes].astype(jnp.float32)
                if roll:
                    ahead = pltpu.roll(value, LANES - 1, 1)
                    around = pltpu.roll(value, X - 1, 1)
                    value = jnp.where(last, around, ahead)
                v.append((value[:half], value[half:]))
            for a in range(3):
                ur, ui = u[0][a], u[1][a]
                outs_r, outs_i = [], []
                for h in range(2):
                    re = [v[b][h] for b in range(3)]
                    im = [v[3 + b][h] for b in range(3)]
                    dr = ur[0] * re[0] - ui[0] * im[0]
                    di = ur[0] * im[0] + ui[0] * re[0]
                    for b in (1, 2):
                        dr = dr + (ur[b] * re[b] - ui[b] * im[b])
                        di = di + (ur[b] * im[b] + ui[b] * re[b])
                    outs_r.append(dr)
                    outs_i.append(di)
                columns = slice(a * sites + t * LANES, a * sites + (t + 1) * LANES)
                to_r = pl.ds(pl.multiple_of(m * ROWS, ROWS), ROWS)
                to_i = pl.ds(pl.multiple_of(count + m * ROWS, ROWS), ROWS)
                d_ref[to_r, columns] = jnp.concatenate(outs_r, axis=0).astype(jnp.bfloat16)
                d_ref[to_i, columns] = jnp.concatenate(outs_i, axis=0).astype(jnp.bfloat16)
            return carry

        lax.fori_loop(0, count // ROWS, body, 0, unroll=2)


def kernel(roll, first, last, start, odd_ref, *refs):
    refs = list(refs)
    left_hbm = refs.pop(0)
    face_ref = None if roll else refs.pop(0)
    u_ref = refs.pop(0)
    acc_hbm = None if first else refs.pop(0)
    outs = [refs.pop(0) for _ in range(2 if last else 1)]
    left, d_ref, acc, sems = refs[:4]
    count, sites = left_hbm.shape[1:]
    n = d_ref.shape[0] // 2
    j = slice(start, start + n)

    if roll:
        face_ref = refs[4]
        copy_field = pltpu.make_async_copy(left_hbm, face_ref, sems.at[0])
        copy_field.start()
    copies = []
    for part in range(2):
        for a in range(3):
            to = left.at[pl.ds(part * count, count), pl.ds(a * sites, sites)]
            k = part * 3 + a
            copies.append(pltpu.make_async_copy(left_hbm.at[k], to, sems.at[1 + k]))
    if not first:
        copies.append(pltpu.make_async_copy(acc_hbm, acc, sems.at[7]))
    for copy in copies:
        copy.start()
    if roll:
        copy_field.wait()
    displace(face_ref, u_ref, d_ref, roll)
    for copy in copies:
        copy.wait()

    product = lax.dot_general(
        left[...], d_ref[...], (((1,), (1,)), ((), ())), preferred_element_type=jnp.float32
    )
    sum_re = product[:count, :n] + product[count:, n:]
    sum_im = product[:count, n:] - product[count:, :n]
    if n == count:
        acc[0] = sum_re - sum_re.T
        acc[1] = sum_im + sum_im.T
    else:
        if first:
            acc[...] = jnp.zeros_like(acc)
        acc[0, :, j] += sum_re
        acc[1, :, j] += sum_im
        acc[0, j, :] -= sum_re.T
        acc[1, j, :] += sum_im.T
    if last:
        send, keep = outs
        odd = odd_ref[0]
        send[...] = acc[1 - odd].astype(jnp.bfloat16)
        keep[...] = acc[odd]
    else:
        outs[0][...] = acc[...]


def direction(odd, left, field, u, acc, start, n, last):
    count, sites = left.shape[1:]
    roll = field is None
    first = acc is None
    operands = [odd, left] + ([] if roll else [field]) + [u] + ([] if first else [acc])
    anywhere = pl.BlockSpec(memory_space=pl.ANY)
    vmem = pl.BlockSpec(memory_space=pltpu.VMEM)
    specs = [pl.BlockSpec(memory_space=pltpu.SMEM), anywhere] + ([] if roll else [vmem]) + [vmem]
    specs += [] if first else [anywhere]
    if last:
        shape = [
            jax.ShapeDtypeStruct((count, count), jnp.bfloat16),
            jax.ShapeDtypeStruct((count, count), jnp.float32),
        ]
    else:
        shape = [jax.ShapeDtypeStruct((2, count, count), jnp.float32)]
    return pl.pallas_call(
        functools.partial(kernel, roll, first, last, start),
        out_shape=shape,
        in_specs=specs,
        out_specs=[vmem] * len(shape),
        scratch_shapes=[
            pltpu.VMEM((2 * count, 3 * sites), jnp.bfloat16),
            pltpu.VMEM((2 * n, 3 * sites), jnp.bfloat16),
            pltpu.VMEM((2, count, count), jnp.float32),
            pltpu.SemaphoreType.DMA((8,)),
        ]
        + [pltpu.VMEM((6, n, sites), jnp.bfloat16)] * roll,
        compiler_params=pltpu.CompilerParams(vmem_limit_bytes=40 * 2**20),
        cost_estimate=pl.CostEstimate(
            flops=8 * count * n * 3 * sites,
            bytes_accessed=20 * count * sites,
            transcendentals=0,
        ),
    )(*operands)


def shards(vectors, links):
    slabs = lax.axis_size("gz")
    count, planes, sites = vectors.shape[1], vectors.shape[3], vectors.shape[4]
    assert planes == 1 and slabs % 2 == 0
    own = count // slabs
    scale = 1.0 / math.sqrt(12.0 * sites * planes * slabs)
    odd = (lax.axis_index("gz") % 2).astype(jnp.int32).reshape(1)
    field = jnp.transpose(vectors, (0, 2, 3, 1, 4)).reshape(6, count, sites)
    n = count // CHUNKS
    faces = [passed_along(field[:, c * n : (c + 1) * n], "gz", -1) for c in range(CHUNKS)]
    links_x = links[:, 0].reshape(18, sites)
    links_z = links[:, 1].reshape(18, sites)

    def exchanged(send, keep):
        chip = (keep + swapped(send, "gz").astype(jnp.float32)).astype(jnp.bfloat16)
        got = lax.all_to_all(chip.reshape(slabs, own, count), "gz", 0, 0)
        got = got.reshape(slabs // 2, 2, own, count)
        return jnp.sum(got.astype(jnp.float32), axis=0)

    sum_x = exchanged(*direction(odd, field, None, links_x, None, 0, count, True))
    acc = None
    for c, face in enumerate(faces):
        out = direction(odd, field, face, links_z, acc, c * n, n, c == CHUNKS - 1)
        acc = out[0]
    sum_z = exchanged(*out)
    both = jnp.concatenate([sum_x, sum_z], axis=0)
    return jnp.transpose(both, (1, 0, 2)) * scale


def solution(mesh):
    return jax.shard_map(
        shards,
        mesh=mesh,
        in_specs=(P("grp", None, None, "gz", None), P("grp", None, None, None, "gz", None)),
        out_specs=P("gz", "grp", None),
        check_vma=False,
    )
```

```python
import functools
import math

import jax
import jax.numpy as jnp
from jax import lax
from jax.experimental import pallas as pl
from jax.experimental.pallas import tpu as pltpu
from jax.sharding import PartitionSpec as P

X = 64
LANES = 128
ROWS = 16
VMEM = pl.BlockSpec(memory_space=pltpu.VMEM)
SMEM = pl.BlockSpec(memory_space=pltpu.SMEM)


def passed_along(block, axis, distance):
    devices = range(lax.axis_size(axis))
    route = [((i - distance) % len(devices), i) for i in devices]
    return lax.ppermute(block, axis, route)


def swapped(block, axis):
    return lax.ppermute(block, axis, [(i, i ^ 1) for i in range(lax.axis_size(axis))])


def displace(field_ref, links_ref, mu, a, d_ref, roll):
    sites = field_ref.shape[2]
    n = field_ref.shape[1]
    half = ROWS // 2
    for t in range(sites // LANES):
        lanes = slice(t * LANES, (t + 1) * LANES)

        def link(part, b):
            row = ((part * 2 + mu) * 3 + a) * 3 + b
            return jnp.broadcast_to(links_ref[row : row + 1, lanes], (half, LANES))

        ur = [link(0, b) for b in range(3)]
        ui = [link(1, b) for b in range(3)]
        if roll:
            lane = lax.broadcasted_iota(jnp.int32, (half, LANES), 1)
            last = (lane & (X - 1)) == X - 1

        def around(value):
            return jnp.where(last, pltpu.roll(value, X - 1, 1), pltpu.roll(value, LANES - 1, 1))

        def body(m, carry):
            first = m * ROWS if isinstance(m, int) else pl.multiple_of(m * ROWS, ROWS)
            v = [field_ref[k, pl.ds(first, ROWS), lanes].astype(jnp.float32) for k in range(6)]
            outs_r, outs_i = [], []
            for h in range(2):
                rows = slice(h * half, (h + 1) * half)
                re = [v[b][rows] for b in range(3)]
                im = [v[3 + b][rows] for b in range(3)]
                if roll:
                    re, im = [around(r) for r in re], [around(i) for i in im]
                dr = ur[0] * re[0] - ui[0] * im[0]
                di = ur[0] * im[0] + ui[0] * re[0]
                for b in (1, 2):
                    dr = dr + (ur[b] * re[b] - ui[b] * im[b])
                    di = di + (ur[b] * im[b] + ui[b] * re[b])
                outs_r.append(dr)
                outs_i.append(di)
            d_ref[pl.ds(first, ROWS), lanes] = jnp.concatenate(outs_r, axis=0).astype(jnp.bfloat16)
            d_ref[pl.ds(n + first, ROWS), lanes] = jnp.concatenate(outs_i, axis=0).astype(jnp.bfloat16)
            return carry

        if n <= LANES:
            for m in range(n // ROWS):
                body(m, 0)
        else:
            lax.fori_loop(0, n // ROWS, body, 0, unroll=4)


def by_halves(slabs, own):
    return own % 8 == 0 and slabs & (slabs - 1) == 0


def halving_order(k, chips):
    bits = chips.bit_length() - 1
    return sum(((k >> b) & 1) << (bits - 1 - b) for b in range(bits))


def kernel(mu, first, last, start, slabs, where_ref, *refs):
    refs = list(refs)
    left_ref = refs.pop(0)
    field_ref = left_ref if mu == 0 else refs.pop(0)
    links_ref = refs.pop(0)
    acc_in = None if first else refs.pop(0)
    outs = [refs.pop(0) for _ in range(2 if last else 1)]
    d_refs = [refs.pop(0) for _ in range(3)]
    acc = refs.pop(0) if last else outs[0]
    count = left_ref.shape[1]
    n = field_ref.shape[1]
    j = slice(start, start + n)

    product = [None, None]
    for a in range(3):
        displace(field_ref, links_ref, mu, a, d_refs[a], mu == 0)
        for part in range(2):
            term = lax.dot_general(
                left_ref[part * 3 + a], d_refs[a][...], (((1,), (1,)), ((), ())),
                preferred_element_type=jnp.float32,
            )
            product[part] = term if a == 0 else product[part] + term
    sum_re = product[0][:, :n] + product[1][:, n:]
    sum_im = product[0][:, n:] - product[1][:, :n]
    if n == count:
        acc[0] = sum_re - sum_re.T
        acc[1] = sum_im + sum_im.T
    else:
        acc[...] = jnp.zeros_like(acc) if first else acc_in[...]
        acc[0, :, j] += sum_re
        acc[1, :, j] += sum_im
        acc[0, j, :] -= sum_re.T
        acc[1, j, :] += sum_im.T
    if not last:
        return
    send, keep = outs
    core, chip = where_ref[0], where_ref[1]
    own = count // slabs
    if not by_halves(slabs, own):
        send[...] = acc[1 - core].astype(jnp.bfloat16)
        keep[...] = acc[core]
        return
    for k in range(slabs // 2):
        if mu == 0:
            to = halving_order(k, slabs // 2) * 2
        else:
            to = lax.rem(chip + k, slabs // 2) * 2
        block = slice(k * 2 * own, (k + 1) * 2 * own)

        def rows(which):
            at = pl.ds(pl.multiple_of((to + which) * own, 8), own)
            return jnp.concatenate([acc[0, at, :], acc[1, at, :]], axis=0)

        send[block, :] = rows(1 - core).astype(jnp.bfloat16)
        keep[block, :] = rows(core)


def direction(where, left, field, links, acc, start, n, last, slabs):
    count, sites = left.shape[1:]
    mu = 0 if field is None else 1
    first = acc is None
    operands = [where, left] + [field] * mu + [links] + ([] if first else [acc])
    square = (2, count, count)
    if last:
        shape = [
            jax.ShapeDtypeStruct((count, count), jnp.bfloat16),
            jax.ShapeDtypeStruct((count, count), jnp.float32),
        ]
    else:
        shape = [jax.ShapeDtypeStruct(square, jnp.float32)]
    return pl.pallas_call(
        functools.partial(kernel, mu, first, last, start, slabs),
        out_shape=shape,
        in_specs=[SMEM] + [VMEM] * (len(operands) - 1),
        out_specs=[VMEM] * len(shape),
        scratch_shapes=[pltpu.VMEM((2 * n, sites), jnp.bfloat16)] * 3
        + [pltpu.VMEM(square, jnp.float32)] * last,
        compiler_params=pltpu.CompilerParams(vmem_limit_bytes=36 * 2**20),
        cost_estimate=pl.CostEstimate(
            flops=8 * count * n * 3 * sites,
            bytes_accessed=12 * count * sites,
            transcendentals=0,
        ),
    )(*operands)


def halve_kernel(bit, where_ref, kept_ref, got_ref, send_ref, keep_ref):
    size = keep_ref.shape[0]
    mine = (where_ref[1] >> bit) & 1

    def total(which):
        rows = pl.ds(pl.multiple_of(which * size, ROWS), size)
        return kept_ref[rows, :] + got_ref[rows, :].astype(jnp.float32)

    send_ref[...] = total(1 - mine).astype(jnp.bfloat16)
    keep_ref[...] = total(mine)


def halved(where, send, keep, slabs):
    for bit in range(slabs.bit_length() - 1):
        got = lax.ppermute(send, "gz", [(i, i ^ (1 << bit)) for i in range(slabs)])
        if bit == slabs.bit_length() - 2:
            return [keep, got]
        half = (send.shape[0] // 2, send.shape[1])
        send, keep = pl.pallas_call(
            functools.partial(halve_kernel, bit),
            out_shape=[
                jax.ShapeDtypeStruct(half, jnp.bfloat16),
                jax.ShapeDtypeStruct(half, jnp.float32),
            ],
            in_specs=[SMEM, VMEM, VMEM],
            out_specs=[VMEM] * 2,
        )(where, keep, got)


def add_kernel(kept_ref, got_ref, own_ref, *block_refs):
    size = own_ref.shape[0]
    own_ref[...] = kept_ref[:size, :] + got_ref[:size, :].astype(jnp.float32)
    for k, ref in enumerate(block_refs):
        rows = slice((k + 1) * size, (k + 2) * size)
        ref[...] = (kept_ref[rows, :] + got_ref[rows, :].astype(jnp.float32)).astype(jnp.bfloat16)


def chips_terms(send, keep, slabs):
    count = send.shape[0]
    block = (count // (slabs // 2), count)
    others = slabs // 2 - 1
    got = swapped(send, "gz")
    mine, *blocks = pl.pallas_call(
        add_kernel,
        out_shape=[jax.ShapeDtypeStruct(block, jnp.float32)]
        + [jax.ShapeDtypeStruct(block, jnp.bfloat16)] * others,
        in_specs=[VMEM] * 2,
        out_specs=[VMEM] * (others + 1),
    )(keep, got)
    return [mine] + [passed_along(b, "gz", 2 * (k + 1)) for k, b in enumerate(blocks)]


def final_kernel(scale, out_ref, x_refs, z_refs):
    own = out_ref.shape[0]
    for m, refs in enumerate((x_refs, z_refs)):
        total = refs[0][...]
        for ref in refs[1:]:
            total = total + ref[...].astype(jnp.float32)
        total = total * scale
        out_ref[:, 2 * m, :] = total[:own]
        out_ref[:, 2 * m + 1, :] = total[own:]


def assembled(terms_x, terms_z, own, scale):
    count = terms_x[0].shape[1]
    n = len(terms_x)
    operands = [*terms_x, *terms_z]

    def body(*refs):
        final_kernel(scale, refs[-1], refs[:n], refs[n:-1])

    return pl.pallas_call(
        body,
        out_shape=jax.ShapeDtypeStruct((own, 4, count), jnp.float32),
        in_specs=[VMEM] * len(operands),
        out_specs=VMEM,
    )(*operands)


def shards(vectors, links):
    slabs = lax.axis_size("gz")
    count, planes, sites = vectors.shape[1], vectors.shape[3], vectors.shape[4]
    assert planes == 1 and slabs % 2 == 0
    own = count // slabs
    scale = 1.0 / math.sqrt(12.0 * sites * planes * slabs)
    index = lax.axis_index("gz").astype(jnp.int32)
    where = jnp.stack([index & 1, index >> 1])
    field = jnp.transpose(vectors, (0, 2, 3, 1, 4)).reshape(6, count, sites)
    links = links.reshape(36, sites)
    starts = [0, count // 6, count // 2, count - count // 6, count]
    faces, rest = [], field
    for low, high in zip(starts, starts[1:]):
        piece = rest[:, low:high]
        faces.append(passed_along(piece, "gz", -1))
        piece, rest = lax.optimization_barrier((piece, rest))

    out_x = direction(where, field, None, links, None, 0, count, True, slabs)
    if by_halves(slabs, own):
        terms_x = halved(where, *out_x, slabs)
        faces[-2], *terms_x = lax.optimization_barrier((faces[-2], *terms_x))
    acc = None
    for c, face in enumerate(faces):
        n = starts[c + 1] - starts[c]
        out_z = direction(where, field, face, links, acc, starts[c], n, c == len(faces) - 1, slabs)
        acc = out_z[0]
    if by_halves(slabs, own):
        return assembled(terms_x, chips_terms(*out_z, slabs), own, scale)

    def exchanged(send, keep):
        chip = (keep + swapped(send, "gz").astype(jnp.float32)).astype(jnp.bfloat16)
        got = lax.all_to_all(chip.reshape(slabs, own, count), "gz", 0, 0)
        got = got.reshape(slabs // 2, 2, own, count)
        return jnp.sum(got.astype(jnp.float32), axis=0)

    both = jnp.concatenate([exchanged(*out_x), exchanged(*out_z)], axis=0)
    return jnp.transpose(both, (1, 0, 2)) * scale


def solution(mesh):
    return jax.shard_map(
        shards,
        mesh=mesh,
        in_specs=(P("grp", None, None, "gz", None), P("grp", None, None, None, "gz", None)),
        out_specs=P("gz", "grp", None),
        check_vma=False,
    )
```

```python
import functools
import math

import jax
import jax.numpy as jnp
from jax import lax
from jax.experimental import pallas as pl
from jax.experimental.pallas import tpu as pltpu
from jax.sharding import PartitionSpec as P

X = 64
LANES = 128
ROWS = 16
VMEM = pl.BlockSpec(memory_space=pltpu.VMEM)
SMEM = pl.BlockSpec(memory_space=pltpu.SMEM)
ANY = pl.BlockSpec(memory_space=pl.ANY)


def passed_along(block, axis, distance):
    devices = range(lax.axis_size(axis))
    route = [((i - distance) % len(devices), i) for i in devices]
    return lax.ppermute(block, axis, route)


def swapped(block, axis):
    return lax.ppermute(block, axis, [(i, i ^ 1) for i in range(lax.axis_size(axis))])


def times_links(field_ref, links_ref, mu, adjoint, roll, store):
    count, sites = field_ref.shape[1:]
    for t in range(sites // LANES):
        lanes = slice(t * LANES, (t + 1) * LANES)

        def link(part, a, b):
            row = ((part * 2 + mu) * 3 + a) * 3 + b
            value = jnp.broadcast_to(links_ref[row : row + 1, lanes], (ROWS, LANES))
            return -value if adjoint and part == 1 else value

        def links_of(part, a):
            return [link(part, b, a) if adjoint else link(part, a, b) for b in range(3)]

        u = [[links_of(p, a) for a in range(3)] for p in range(2)]
        if roll:
            lane = lax.broadcasted_iota(jnp.int32, (ROWS, LANES), 1)
            last = (lane & (X - 1)) == X - 1

        def body(m, carry):
            rows = pl.ds(pl.multiple_of(m * ROWS, ROWS), ROWS)
            v = []
            for k in range(6):
                value = field_ref[k, rows, lanes].astype(jnp.float32)
                if roll:
                    ahead = pltpu.roll(value, LANES - 1, 1)
                    around = pltpu.roll(value, X - 1, 1)
                    value = jnp.where(last, around, ahead)
                v.append(value)
            re, im = v[:3], v[3:]
            for a in range(3):
                ur, ui = u[0][a], u[1][a]
                dr = ur[0] * re[0] - ui[0] * im[0]
                di = ur[0] * im[0] + ui[0] * re[0]
                for b in (1, 2):
                    dr = dr + (ur[b] * re[b] - ui[b] * im[b])
                    di = di + (ur[b] * im[b] + ui[b] * re[b])
                store(0, a, m, lanes, dr.astype(jnp.bfloat16))
                store(1, a, m, lanes, di.astype(jnp.bfloat16))
            return carry

        lax.fori_loop(0, count // ROWS, body, 0, unroll=2)


def rows_by_own(slabs, own):
    return slabs % 2 == 0 and own % 8 == 0


def finish(left_of, right_of, slabs, core, acc, send, keep, ready=lambda b: None):
    count = send.shape[0]
    own = count // slabs
    product = [None, None]
    for b in range(3):
        ready(b)
        for part in range(2):
            term = lax.dot_general(
                left_of(part, b), right_of(b), (((1,), (1,)), ((), ())),
                preferred_element_type=jnp.float32,
            )
            product[part] = term if b == 0 else product[part] + term
    sum_re = product[0][:, :count] + product[1][:, count:]
    sum_im = product[0][:, count:] - product[1][:, :count]
    acc[0] = sum_re - sum_re.T
    acc[1] = sum_im + sum_im.T
    if not rows_by_own(slabs, own):
        send[...] = acc[1 - core].astype(jnp.bfloat16)
        keep[...] = acc[core]
        return
    for k in range(slabs // 2):
        block = slice(k * 2 * own, (k + 1) * 2 * own)

        def rows(which):
            at = pl.ds(pl.multiple_of((2 * k + which) * own, 8), own)
            return jnp.concatenate([acc[0, at, :], acc[1, at, :]], axis=0)

        send[block, :] = rows(1 - core).astype(jnp.bfloat16)
        keep[block, :] = rows(core)


def x_kernel(slabs, core_ref, field_ref, links_ref, send, keep, right, acc):
    count = field_ref.shape[1]

    def store(part, a, m, lanes, value):
        right[a, pl.ds(pl.multiple_of(part * count + m * ROWS, ROWS), ROWS), lanes] = value

    times_links(field_ref, links_ref, 0, False, True, store)
    finish(
        lambda part, b: field_ref[part * 3 + b], lambda b: right[b],
        slabs, core_ref[0], acc, send, keep,
    )


def w_kernel(field_ref, links_ref, w_ref):
    def store(part, a, m, lanes, value):
        w_ref[part * 3 + a, pl.ds(pl.multiple_of(m * ROWS, ROWS), ROWS), lanes] = value

    times_links(field_ref, links_ref, 1, True, False, store)


def z_kernel(slabs, core_ref, w_ref, face_hbm, send, keep, right, acc, sems):
    count = w_ref.shape[1]
    copies = []
    for b in range(3):
        for part in range(2):
            to = right.at[b, pl.ds(part * count, count)]
            k = part * 3 + b
            copies.append(pltpu.make_async_copy(face_hbm.at[k], to, sems.at[k]))
    for copy in copies:
        copy.start()

    def ready(b):
        copies[2 * b].wait()
        copies[2 * b + 1].wait()

    finish(
        lambda part, b: w_ref[part * 3 + b], lambda b: right[b],
        slabs, core_ref[0], acc, send, keep, ready,
    )


def call(body, outs, specs, scratch, mib, flops, moved):
    return pl.pallas_call(
        body,
        out_shape=outs,
        in_specs=specs,
        out_specs=[VMEM] * len(outs),
        scratch_shapes=scratch,
        compiler_params=pltpu.CompilerParams(vmem_limit_bytes=mib * 2**20),
        cost_estimate=pl.CostEstimate(flops=flops, bytes_accessed=moved, transcendentals=0),
    )


def shards(vectors, links):
    slabs = lax.axis_size("gz")
    count, planes, sites = vectors.shape[1], vectors.shape[3], vectors.shape[4]
    assert planes == 1 and slabs % 2 == 0
    own = count // slabs
    scale = 1.0 / math.sqrt(12.0 * sites * planes * slabs)
    core = (lax.axis_index("gz").astype(jnp.int32) & 1).reshape(1)
    field = jnp.transpose(vectors, (0, 2, 3, 1, 4)).reshape(6, count, sites)
    links = links.reshape(36, sites)
    face = passed_along(field, "gz", -1)

    flops = 24 * count * count * sites
    moved = 12 * count * sites
    halves = [
        jax.ShapeDtypeStruct((count, count), jnp.bfloat16),
        jax.ShapeDtypeStruct((count, count), jnp.float32),
    ]
    scratch = [
        pltpu.VMEM((3, 2 * count, sites), jnp.bfloat16),
        pltpu.VMEM((2, count, count), jnp.float32),
    ]
    send_x, keep_x = call(
        functools.partial(x_kernel, slabs), halves, [SMEM, VMEM, VMEM], scratch, 28, flops, moved
    )(core, field, links)
    (w,) = call(
        w_kernel, [jax.ShapeDtypeStruct(field.shape, jnp.bfloat16)], [VMEM, VMEM], [], 16,
        count * sites * 66, 2 * moved,
    )(field, links)

    def exchanged(send, keep):
        chip = (keep + swapped(send, "gz").astype(jnp.float32)).astype(jnp.bfloat16)
        if rows_by_own(slabs, own):
            groups = [list(range(c, slabs, 2)) for c in range(2)]
            chip = chip.reshape(slabs // 2, 2 * own, count)
            got = lax.all_to_all(chip, "gz", 0, 0, axis_index_groups=groups)
            return jnp.sum(got.astype(jnp.float32), axis=0).reshape(2, own, count)
        got = lax.all_to_all(chip.reshape(slabs, own, count), "gz", 0, 0)
        got = got.reshape(slabs // 2, 2, own, count)
        return jnp.sum(got.astype(jnp.float32), axis=0)

    sum_x = exchanged(send_x, keep_x)
    face, sum_x, w = lax.optimization_barrier((face, sum_x, w))
    send_z, keep_z = call(
        functools.partial(z_kernel, slabs), halves, [SMEM, VMEM, ANY],
        scratch + [pltpu.SemaphoreType.DMA((6,))], 28, flops, moved,
    )(core, w, face)
    both = jnp.concatenate([sum_x, exchanged(send_z, keep_z)], axis=0)
    return jnp.transpose(both, (1, 0, 2)) * scale


def solution(mesh):
    return jax.shard_map(
        shards,
        mesh=mesh,
        in_specs=(P("grp", None, None, "gz", None), P("grp", None, None, None, "gz", None)),
        out_specs=P("gz", "grp", None),
        check_vma=False,
    )
```

```python
import functools
import math

import jax
import jax.numpy as jnp
from jax import lax
from jax.experimental import pallas as pl
from jax.experimental.pallas import tpu as pltpu
from jax.sharding import PartitionSpec as P

X = 64
LANES = 128
ROWS = 16
VMEM = pl.BlockSpec(memory_space=pltpu.VMEM)
SMEM = pl.BlockSpec(memory_space=pltpu.SMEM)
ANY = pl.BlockSpec(memory_space=pl.ANY)


def passed_along(block, axis, distance):
    devices = range(lax.axis_size(axis))
    route = [((i - distance) % len(devices), i) for i in devices]
    return lax.ppermute(block, axis, route)


def swapped(block, axis):
    return lax.ppermute(block, axis, [(i, i ^ 1) for i in range(lax.axis_size(axis))])


def times_links(field_ref, links_ref, mu, adjoint, roll, store):
    count, sites = field_ref.shape[1:]
    for t in range(sites // LANES):
        lanes = slice(t * LANES, (t + 1) * LANES)

        def link(part, a, b):
            row = ((part * 2 + mu) * 3 + a) * 3 + b
            value = jnp.broadcast_to(links_ref[row : row + 1, lanes], (ROWS, LANES))
            return -value if adjoint and part == 1 else value

        def links_of(part, a):
            return [link(part, b, a) if adjoint else link(part, a, b) for b in range(3)]

        u = [[links_of(p, a) for a in range(3)] for p in range(2)]
        if roll:
            lane = lax.broadcasted_iota(jnp.int32, (ROWS, LANES), 1)
            last = (lane & (X - 1)) == X - 1

        def body(m, carry):
            rows = pl.ds(pl.multiple_of(m * ROWS, ROWS), ROWS)
            v = []
            for k in range(6):
                value = field_ref[k, rows, lanes].astype(jnp.float32)
                if roll:
                    ahead = pltpu.roll(value, LANES - 1, 1)
                    around = pltpu.roll(value, X - 1, 1)
                    value = jnp.where(last, around, ahead)
                v.append(value)
            re, im = v[:3], v[3:]
            for a in range(3):
                ur, ui = u[0][a], u[1][a]
                dr = ur[0] * re[0] - ui[0] * im[0]
                di = ur[0] * im[0] + ui[0] * re[0]
                for b in (1, 2):
                    dr = dr + (ur[b] * re[b] - ui[b] * im[b])
                    di = di + (ur[b] * im[b] + ui[b] * re[b])
                store(0, a, m, lanes, dr.astype(jnp.bfloat16))
                store(1, a, m, lanes, di.astype(jnp.bfloat16))
            return carry

        lax.fori_loop(0, count // ROWS, body, 0, unroll=2)


def rows_by_own(slabs, own):
    return slabs % 2 == 0 and own % 8 == 0


def finish(left_of, right_of, slabs, core, acc, send, keep, ready=lambda b: None):
    count = send.shape[0]
    own = count // slabs
    product = [None, None]
    for b in range(3):
        ready(b)
        for part in range(2):
            term = lax.dot_general(
                left_of(part, b), right_of(b), (((1,), (1,)), ((), ())),
                preferred_element_type=jnp.float32,
            )
            product[part] = term if b == 0 else product[part] + term
    sum_re = product[0][:, :count] + product[1][:, count:]
    sum_im = product[0][:, count:] - product[1][:, :count]
    acc[0] = sum_re - sum_re.T
    acc[1] = sum_im + sum_im.T
    if not rows_by_own(slabs, own):
        send[...] = acc[1 - core].astype(jnp.bfloat16)
        keep[...] = acc[core]
        return
    for k in range(slabs // 2):
        block = slice(k * 2 * own, (k + 1) * 2 * own)

        def rows(which):
            at = pl.ds(pl.multiple_of((2 * k + which) * own, 8), own)
            return jnp.concatenate([acc[0, at, :], acc[1, at, :]], axis=0)

        send[block, :] = rows(1 - core).astype(jnp.bfloat16)
        keep[block, :] = rows(core)


def x_kernel(slabs, core_ref, field_ref, links_ref, send, keep, right, acc):
    count = field_ref.shape[1]

    def store(part, a, m, lanes, value):
        right[a, pl.ds(pl.multiple_of(part * count + m * ROWS, ROWS), ROWS), lanes] = value

    times_links(field_ref, links_ref, 0, False, True, store)
    finish(
        lambda part, b: field_ref[part * 3 + b], lambda b: right[b],
        slabs, core_ref[0], acc, send, keep,
    )


def w_kernel(field_ref, links_ref, w_ref):
    def store(part, a, m, lanes, value):
        w_ref[part * 3 + a, pl.ds(pl.multiple_of(m * ROWS, ROWS), ROWS), lanes] = value

    times_links(field_ref, links_ref, 1, True, False, store)


def z_kernel(slabs, core_ref, w_ref, face_hbm, send, keep, right, acc, sems):
    count = w_ref.shape[1]
    copies = []
    for b in range(3):
        for part in range(2):
            to = right.at[b, pl.ds(part * count, count)]
            k = part * 3 + b
            copies.append(pltpu.make_async_copy(face_hbm.at[k], to, sems.at[k]))
    for copy in copies:
        copy.start()

    def ready(b):
        copies[2 * b].wait()
        copies[2 * b + 1].wait()

    finish(
        lambda part, b: w_ref[part * 3 + b], lambda b: right[b],
        slabs, core_ref[0], acc, send, keep, ready,
    )


def call(body, outs, specs, scratch, mib, flops, moved):
    return pl.pallas_call(
        body,
        out_shape=outs,
        in_specs=specs,
        out_specs=[VMEM] * len(outs),
        scratch_shapes=scratch,
        compiler_params=pltpu.CompilerParams(vmem_limit_bytes=mib * 2**20),
        cost_estimate=pl.CostEstimate(flops=flops, bytes_accessed=moved, transcendentals=0),
    )


def shards(vectors, links):
    slabs = lax.axis_size("gz")
    count, planes, sites = vectors.shape[1], vectors.shape[3], vectors.shape[4]
    assert planes == 1 and slabs % 2 == 0
    own = count // slabs
    scale = 1.0 / math.sqrt(12.0 * sites * planes * slabs)
    core = (lax.axis_index("gz").astype(jnp.int32) & 1).reshape(1)
    field = jnp.transpose(vectors, (0, 2, 3, 1, 4)).reshape(6, count, sites)
    links = links.reshape(36, sites)
    face = passed_along(field, "gz", -1)

    flops = 24 * count * count * sites
    moved = 12 * count * sites
    halves = [
        jax.ShapeDtypeStruct((count, count), jnp.bfloat16),
        jax.ShapeDtypeStruct((count, count), jnp.float32),
    ]
    scratch = [
        pltpu.VMEM((3, 2 * count, sites), jnp.bfloat16),
        pltpu.VMEM((2, count, count), jnp.float32),
    ]
    send_x, keep_x = call(
        functools.partial(x_kernel, slabs), halves, [SMEM, VMEM, VMEM], scratch, 22, flops, moved
    )(core, field, links)
    (w,) = call(
        w_kernel, [jax.ShapeDtypeStruct(field.shape, jnp.bfloat16)], [VMEM, VMEM], [], 12,
        count * sites * 66, 2 * moved,
    )(field, links)

    def exchanged(send, keep):
        chip = (keep + swapped(send, "gz").astype(jnp.float32)).astype(jnp.bfloat16)
        if rows_by_own(slabs, own):
            groups = [list(range(c, slabs, 2)) for c in range(2)]
            chip = chip.reshape(slabs // 2, 2 * own, count)
            got = lax.all_to_all(chip, "gz", 0, 0, axis_index_groups=groups)
            return jnp.sum(got.astype(jnp.float32), axis=0).reshape(2, own, count)
        got = lax.all_to_all(chip.reshape(slabs, own, count), "gz", 0, 0)
        got = got.reshape(slabs // 2, 2, own, count)
        return jnp.sum(got.astype(jnp.float32), axis=0)

    sum_x = exchanged(send_x, keep_x)
    send_z, keep_z = call(
        functools.partial(z_kernel, slabs), halves, [SMEM, VMEM, ANY],
        scratch + [pltpu.SemaphoreType.DMA((6,))], 18, flops, moved,
    )(core, w, face)
    both = jnp.concatenate([sum_x, exchanged(send_z, keep_z)], axis=0)
    return jnp.transpose(both, (1, 0, 2)) * scale


def solution(mesh):
    return jax.shard_map(
        shards,
        mesh=mesh,
        in_specs=(P("grp", None, None, "gz", None), P("grp", None, None, None, "gz", None)),
        out_specs=P("gz", "grp", None),
        check_vma=False,
    )
```

```python
import functools
import math

import jax
import jax.numpy as jnp
from jax import lax
from jax.experimental import pallas as pl
from jax.experimental.pallas import tpu as pltpu
from jax.sharding import PartitionSpec as P

X = 64
LANES = 128
ROWS = 16
VMEM = pl.BlockSpec(memory_space=pltpu.VMEM)
SMEM = pl.BlockSpec(memory_space=pltpu.SMEM)
ANY = pl.BlockSpec(memory_space=pl.ANY)


def passed_along(block, axis, distance):
    devices = range(lax.axis_size(axis))
    route = [((i - distance) % len(devices), i) for i in devices]
    return lax.ppermute(block, axis, route)


def swapped(block, axis):
    return lax.ppermute(block, axis, [(i, i ^ 1) for i in range(lax.axis_size(axis))])


def times_links(field_ref, links_ref, mu, adjoint, roll, store):
    count, sites = field_ref.shape[1:]
    for t in range(sites // LANES):
        lanes = slice(t * LANES, (t + 1) * LANES)

        def link(part, a, b):
            row = ((part * 2 + mu) * 3 + a) * 3 + b
            value = jnp.broadcast_to(links_ref[row : row + 1, lanes], (ROWS, LANES))
            return -value if adjoint and part == 1 else value

        def links_of(part, a):
            return [link(part, b, a) if adjoint else link(part, a, b) for b in range(3)]

        u = [[links_of(p, a) for a in range(3)] for p in range(2)]
        if roll:
            lane = lax.broadcasted_iota(jnp.int32, (ROWS, LANES), 1)
            last = (lane & (X - 1)) == X - 1

        def body(m, carry):
            rows = pl.ds(pl.multiple_of(m * ROWS, ROWS), ROWS)
            v = []
            for k in range(6):
                value = field_ref[k, rows, lanes].astype(jnp.float32)
                if roll:
                    ahead = pltpu.roll(value, LANES - 1, 1)
                    around = pltpu.roll(value, X - 1, 1)
                    value = jnp.where(last, around, ahead)
                v.append(value)
            re, im = v[:3], v[3:]
            for a in range(3):
                ur, ui = u[0][a], u[1][a]
                dr = ur[0] * re[0] - ui[0] * im[0]
                di = ur[0] * im[0] + ui[0] * re[0]
                for b in (1, 2):
                    dr = dr + (ur[b] * re[b] - ui[b] * im[b])
                    di = di + (ur[b] * im[b] + ui[b] * re[b])
                store(0, a, m, lanes, dr.astype(jnp.bfloat16))
                store(1, a, m, lanes, di.astype(jnp.bfloat16))
            return carry

        lax.fori_loop(0, count // ROWS, body, 0, unroll=2)


def rows_by_own(slabs, own):
    return slabs % 2 == 0 and own % 8 == 0


def finish(left_of, right_of, slabs, core, acc, send, keep, ready=lambda b: None):
    count = send.shape[0]
    own = count // slabs
    product = [None, None]
    for b in range(3):
        ready(b)
        for part in range(2):
            term = lax.dot_general(
                left_of(part, b), right_of(b), (((1,), (1,)), ((), ())),
                preferred_element_type=jnp.float32,
            )
            product[part] = term if b == 0 else product[part] + term
    sum_re = product[0][:, :count] + product[1][:, count:]
    sum_im = product[0][:, count:] - product[1][:, :count]
    acc[0] = sum_re - sum_re.T
    acc[1] = sum_im + sum_im.T
    if not rows_by_own(slabs, own):
        send[...] = acc[1 - core].astype(jnp.bfloat16)
        keep[...] = acc[core]
        return
    for k in range(slabs // 2):
        block = slice(k * 2 * own, (k + 1) * 2 * own)

        def rows(which):
            at = pl.ds(pl.multiple_of((2 * k + which) * own, 8), own)
            return jnp.concatenate([acc[0, at, :], acc[1, at, :]], axis=0)

        send[block, :] = rows(1 - core).astype(jnp.bfloat16)
        keep[block, :] = rows(core)


def x_kernel(slabs, core_ref, field_ref, links_ref, send, keep, right, acc):
    count = field_ref.shape[1]

    def store(part, a, m, lanes, value):
        right[a, pl.ds(pl.multiple_of(part * count + m * ROWS, ROWS), ROWS), lanes] = value

    times_links(field_ref, links_ref, 0, False, True, store)
    finish(
        lambda part, b: field_ref[part * 3 + b], lambda b: right[b],
        slabs, core_ref[0], acc, send, keep,
    )


def w_kernel(field_ref, links_ref, keep_ref, got_ref, w_ref, chip_ref):
    chip_ref[...] = (keep_ref[...] + got_ref[...].astype(jnp.float32)).astype(jnp.bfloat16)

    def store(part, a, m, lanes, value):
        w_ref[part * 3 + a, pl.ds(pl.multiple_of(m * ROWS, ROWS), ROWS), lanes] = value

    times_links(field_ref, links_ref, 1, True, False, store)


def z_kernel(slabs, core_ref, w_ref, face_hbm, send, keep, right, acc, sems):
    count = w_ref.shape[1]
    copies = []
    for b in range(3):
        for part in range(2):
            to = right.at[b, pl.ds(part * count, count)]
            k = part * 3 + b
            copies.append(pltpu.make_async_copy(face_hbm.at[k], to, sems.at[k]))
    for copy in copies:
        copy.start()

    def ready(b):
        copies[2 * b].wait()
        copies[2 * b + 1].wait()

    finish(
        lambda part, b: w_ref[part * 3 + b], lambda b: right[b],
        slabs, core_ref[0], acc, send, keep, ready,
    )


def call(body, outs, specs, scratch, mib, flops, moved):
    return pl.pallas_call(
        body,
        out_shape=outs,
        in_specs=specs,
        out_specs=[VMEM] * len(outs),
        scratch_shapes=scratch,
        compiler_params=pltpu.CompilerParams(vmem_limit_bytes=mib * 2**20),
        cost_estimate=pl.CostEstimate(flops=flops, bytes_accessed=moved, transcendentals=0),
    )


def shards(vectors, links):
    slabs = lax.axis_size("gz")
    count, planes, sites = vectors.shape[1], vectors.shape[3], vectors.shape[4]
    assert planes == 1 and slabs % 2 == 0
    own = count // slabs
    scale = 1.0 / math.sqrt(12.0 * sites * planes * slabs)
    core = (lax.axis_index("gz").astype(jnp.int32) & 1).reshape(1)
    field = jnp.transpose(vectors, (0, 2, 3, 1, 4)).reshape(6, count, sites)
    links = links.reshape(36, sites)
    face = passed_along(field, "gz", -1)

    flops = 24 * count * count * sites
    moved = 12 * count * sites
    halves = [
        jax.ShapeDtypeStruct((count, count), jnp.bfloat16),
        jax.ShapeDtypeStruct((count, count), jnp.float32),
    ]
    scratch = [
        pltpu.VMEM((3, 2 * count, sites), jnp.bfloat16),
        pltpu.VMEM((2, count, count), jnp.float32),
    ]
    send_x, keep_x = call(
        functools.partial(x_kernel, slabs), halves, [SMEM, VMEM, VMEM], scratch, 22, flops, moved
    )(core, field, links)
    w, chip_x = call(
        w_kernel, [jax.ShapeDtypeStruct(field.shape, jnp.bfloat16), halves[0]], [VMEM] * 4, [], 12,
        count * sites * 66, 2 * moved,
    )(field, links, keep_x, swapped(send_x, "gz"))

    def exchanged(chip):
        if rows_by_own(slabs, own):
            groups = [list(range(c, slabs, 2)) for c in range(2)]
            chip = chip.reshape(slabs // 2, 2 * own, count)
            got = lax.psum_scatter(chip, "gz", scatter_dimension=0, axis_index_groups=groups)
            return got.astype(jnp.float32).reshape(2, own, count)
        got = lax.all_to_all(chip.reshape(slabs, own, count), "gz", 0, 0)
        got = got.reshape(slabs // 2, 2, own, count)
        return jnp.sum(got.astype(jnp.float32), axis=0)

    sum_x = exchanged(chip_x)
    core, sum_x = lax.optimization_barrier((core, sum_x))
    send_z, keep_z = call(
        functools.partial(z_kernel, slabs), halves, [SMEM, VMEM, ANY],
        scratch + [pltpu.SemaphoreType.DMA((6,))], 18, flops, moved,
    )(core, w, face)
    chip_z = (keep_z + swapped(send_z, "gz").astype(jnp.float32)).astype(jnp.bfloat16)
    both = jnp.concatenate([sum_x, exchanged(chip_z)], axis=0)
    return jnp.transpose(both, (1, 0, 2)) * scale


def solution(mesh):
    return jax.shard_map(
        shards,
        mesh=mesh,
        in_specs=(P("grp", None, None, "gz", None), P("grp", None, None, None, "gz", None)),
        out_specs=P("gz", "grp", None),
        check_vma=False,
    )
```

```python
import functools
import math

import jax
import jax.numpy as jnp
from jax import lax
from jax.experimental import pallas as pl
from jax.experimental.pallas import tpu as pltpu
from jax.sharding import PartitionSpec as P

X = 64
LANES = 128
ROWS = 16
VMEM = pl.BlockSpec(memory_space=pltpu.VMEM)
SMEM = pl.BlockSpec(memory_space=pltpu.SMEM)
ANY = pl.BlockSpec(memory_space=pl.ANY)


def passed_along(block, axis, distance):
    devices = range(lax.axis_size(axis))
    route = [((i - distance) % len(devices), i) for i in devices]
    return lax.ppermute(block, axis, route)


def swapped(block, axis):
    return lax.ppermute(block, axis, [(i, i ^ 1) for i in range(lax.axis_size(axis))])


def times_links(field_ref, links_ref, mu, adjoint, roll, store):
    count, sites = field_ref.shape[1:]
    for t in range(sites // LANES):
        lanes = slice(t * LANES, (t + 1) * LANES)

        def link(part, a, b):
            row = ((part * 2 + mu) * 3 + a) * 3 + b
            value = jnp.broadcast_to(links_ref[row : row + 1, lanes], (ROWS, LANES))
            return -value if adjoint and part == 1 else value

        def links_of(part, a):
            return [link(part, b, a) if adjoint else link(part, a, b) for b in range(3)]

        u = [[links_of(p, a) for a in range(3)] for p in range(2)]
        if roll:
            lane = lax.broadcasted_iota(jnp.int32, (ROWS, LANES), 1)
            last = (lane & (X - 1)) == X - 1

        def body(m, carry):
            rows = pl.ds(pl.multiple_of(m * ROWS, ROWS), ROWS)
            v = []
            for k in range(6):
                value = field_ref[k, rows, lanes].astype(jnp.float32)
                if roll:
                    ahead = pltpu.roll(value, LANES - 1, 1)
                    around = pltpu.roll(value, X - 1, 1)
                    value = jnp.where(last, around, ahead)
                v.append(value)
            re, im = v[:3], v[3:]
            for a in range(3):
                ur, ui = u[0][a], u[1][a]
                dr = ur[0] * re[0] - ui[0] * im[0]
                di = ur[0] * im[0] + ui[0] * re[0]
                for b in (1, 2):
                    dr = dr + (ur[b] * re[b] - ui[b] * im[b])
                    di = di + (ur[b] * im[b] + ui[b] * re[b])
                store(0, a, m, lanes, dr.astype(jnp.bfloat16))
                store(1, a, m, lanes, di.astype(jnp.bfloat16))
            return carry

        lax.fori_loop(0, count // ROWS, body, 0, unroll=2)


def rows_by_own(slabs, own):
    return slabs % 2 == 0 and own % 8 == 0


def inner(left, right):
    return lax.dot_general(left, right, (((1,), (1,)), ((), ())), preferred_element_type=jnp.float32)


def finish(sum_re, sum_im, slabs, core, acc, send, keep):
    count = send.shape[0]
    own = count // slabs
    acc[0] = sum_re - sum_re.T
    acc[1] = sum_im + sum_im.T
    if not rows_by_own(slabs, own):
        send[...] = acc[1 - core].astype(jnp.bfloat16)
        keep[...] = acc[core]
        return
    for k in range(slabs // 2):
        block = slice(k * 2 * own, (k + 1) * 2 * own)

        def rows(which):
            at = pl.ds(pl.multiple_of((2 * k + which) * own, 8), own)
            return jnp.concatenate([acc[0, at, :], acc[1, at, :]], axis=0)

        send[block, :] = rows(1 - core).astype(jnp.bfloat16)
        keep[block, :] = rows(core)


def x_kernel(slabs, core_ref, field_ref, links_ref, send, keep, right, acc):
    count = field_ref.shape[1]

    def store(part, a, m, lanes, value):
        right[a, pl.ds(pl.multiple_of(part * count + m * ROWS, ROWS), ROWS), lanes] = value

    times_links(field_ref, links_ref, 0, False, True, store)
    product = [None, None]
    for b in range(3):
        for part in range(2):
            term = inner(field_ref[part * 3 + b], right[b])
            product[part] = term if b == 0 else product[part] + term
    sum_re = product[0][:, :count] + product[1][:, count:]
    sum_im = product[0][:, count:] - product[1][:, :count]
    finish(sum_re, sum_im, slabs, core_ref[0], acc, send, keep)


def w_kernel(field_ref, links_ref, keep_ref, got_ref, w_ref, chip_ref):
    count, sites = field_ref.shape[1:]
    chip_ref[...] = (keep_ref[...] + got_ref[...].astype(jnp.float32)).astype(jnp.bfloat16)

    def store(part, a, m, lanes, value):
        rows = pl.ds(pl.multiple_of(part * count + m * ROWS, ROWS), ROWS)
        w_ref[rows, slice(a * sites + lanes.start, a * sites + lanes.stop)] = value

    times_links(field_ref, links_ref, 1, True, False, store)


def z_kernel(slabs, core_ref, w_ref, face_hbm, send, keep, right, product, acc, sems):
    count, sites = face_hbm.shape[1:]
    tile = 2 * LANES
    tiles = []
    for low in range(0, 2 * count, tile):
        copies = []
        for part in range(2):
            start, stop = max(low, part * count), min(low + tile, (part + 1) * count)
            for b in range(3 if start < stop else 0):
                to = right.at[pl.ds(start, stop - start), pl.ds(b * sites, sites)]
                of = face_hbm.at[part * 3 + b, pl.ds(start - part * count, stop - start)]
                copies.append(pltpu.make_async_copy(of, to, sems.at[(low // tile) * 6 + part * 3 + b]))
        for copy in copies:
            copy.start()
        tiles.append((slice(low, min(low + tile, 2 * count)), copies))
    for rows, copies in tiles:
        for copy in copies:
            copy.wait()
        product[:, rows] = inner(w_ref[...], right[rows, :])
    sum_re = product[:count, :count] + product[count:, count:]
    sum_im = product[:count, count:] - product[count:, :count]
    finish(sum_re, sum_im, slabs, core_ref[0], acc, send, keep)


def call(body, outs, specs, scratch, mib, flops, moved):
    return pl.pallas_call(
        body,
        out_shape=outs,
        in_specs=specs,
        out_specs=[VMEM] * len(outs),
        scratch_shapes=scratch,
        compiler_params=pltpu.CompilerParams(vmem_limit_bytes=mib * 2**20),
        cost_estimate=pl.CostEstimate(flops=flops, bytes_accessed=moved, transcendentals=0),
    )


def shards(vectors, links):
    slabs = lax.axis_size("gz")
    count, planes, sites = vectors.shape[1], vectors.shape[3], vectors.shape[4]
    assert planes == 1 and slabs % 2 == 0
    own = count // slabs
    scale = 1.0 / math.sqrt(12.0 * sites * planes * slabs)
    core = (lax.axis_index("gz").astype(jnp.int32) & 1).reshape(1)
    field = jnp.transpose(vectors, (0, 2, 3, 1, 4)).reshape(6, count, sites)
    links = links.reshape(36, sites)
    face = passed_along(field, "gz", -1)

    flops = 24 * count * count * sites
    moved = 12 * count * sites
    halves = [
        jax.ShapeDtypeStruct((count, count), jnp.bfloat16),
        jax.ShapeDtypeStruct((count, count), jnp.float32),
    ]
    whole = (2 * count, 3 * sites)
    square = pltpu.VMEM((2, count, count), jnp.float32)
    send_x, keep_x = call(
        functools.partial(x_kernel, slabs), halves, [SMEM, VMEM, VMEM],
        [pltpu.VMEM((3, 2 * count, sites), jnp.bfloat16), square], 22, flops, moved,
    )(core, field, links)
    w, chip_x = call(
        w_kernel, [jax.ShapeDtypeStruct(whole, jnp.bfloat16), halves[0]], [VMEM] * 4, [], 12,
        count * sites * 66, 2 * moved,
    )(field, links, keep_x, swapped(send_x, "gz"))

    if rows_by_own(slabs, own):
        groups = [list(range(c, slabs, 2)) for c in range(2)]
        blocks = (slabs // 2, 1, 2 * own, count)
    else:
        groups = None
        blocks = (slabs // 2, 2, own, count)

    def exchanged(chip):
        chip = chip.reshape((-1,) + blocks[2:])
        return lax.all_to_all(chip, "gz", 0, 0, axis_index_groups=groups)

    def total(got):
        return jnp.sum(got.reshape(blocks).astype(jnp.float32), axis=0).reshape(2, own, count)

    got_x = exchanged(chip_x)
    send_z, keep_z = call(
        functools.partial(z_kernel, slabs), halves, [SMEM, VMEM, ANY],
        [
            pltpu.VMEM(whole, jnp.bfloat16),
            pltpu.VMEM((2 * count, 2 * count), jnp.float32),
            square,
            pltpu.SemaphoreType.DMA((6 * -(-count // LANES),)),
        ],
        20, flops, moved,
    )(core, w, face)
    send_z, got_x = lax.optimization_barrier((send_z, got_x))
    chip_z = (keep_z + swapped(send_z, "gz").astype(jnp.float32)).astype(jnp.bfloat16)
    both = jnp.concatenate([total(got_x), total(exchanged(chip_z))], axis=0)
    return jnp.transpose(both, (1, 0, 2)) * scale


def solution(mesh):
    return jax.shard_map(
        shards,
        mesh=mesh,
        in_specs=(P("grp", None, None, "gz", None), P("grp", None, None, None, "gz", None)),
        out_specs=P("gz", "grp", None),
        check_vma=False,
    )
```

```python
import functools
import math

import jax
import jax.numpy as jnp
from jax import lax
from jax.experimental import pallas as pl
from jax.experimental.pallas import tpu as pltpu
from jax.sharding import PartitionSpec as P

X = 64
LANES = 128
ROWS = 16
VMEM = pl.BlockSpec(memory_space=pltpu.VMEM)
SMEM = pl.BlockSpec(memory_space=pltpu.SMEM)
ANY = pl.BlockSpec(memory_space=pl.ANY)


def passed_along(block, axis, distance):
    devices = range(lax.axis_size(axis))
    route = [((i - distance) % len(devices), i) for i in devices]
    return lax.ppermute(block, axis, route)


def swapped(block, axis):
    return lax.ppermute(block, axis, [(i, i ^ 1) for i in range(lax.axis_size(axis))])


def times_links(field_ref, links_ref, mu, adjoint, roll, store):
    count, sites = field_ref.shape[1:]
    for t in range(sites // LANES):
        lanes = slice(t * LANES, (t + 1) * LANES)

        def link(part, a, b):
            row = ((part * 2 + mu) * 3 + a) * 3 + b
            value = jnp.broadcast_to(links_ref[row : row + 1, lanes], (ROWS, LANES))
            return -value if adjoint and part == 1 else value

        def links_of(part, a):
            return [link(part, b, a) if adjoint else link(part, a, b) for b in range(3)]

        u = [[links_of(p, a) for a in range(3)] for p in range(2)]
        if roll:
            lane = lax.broadcasted_iota(jnp.int32, (ROWS, LANES), 1)
            last = (lane & (X - 1)) == X - 1

        def body(m, carry):
            rows = pl.ds(pl.multiple_of(m * ROWS, ROWS), ROWS)
            v = []
            for k in range(6):
                value = field_ref[k, rows, lanes].astype(jnp.float32)
                if roll:
                    ahead = pltpu.roll(value, LANES - 1, 1)
                    around = pltpu.roll(value, X - 1, 1)
                    value = jnp.where(last, around, ahead)
                v.append(value)
            re, im = v[:3], v[3:]
            for a in range(3):
                ur, ui = u[0][a], u[1][a]
                dr = ur[0] * re[0] - ui[0] * im[0]
                di = ur[0] * im[0] + ui[0] * re[0]
                for b in (1, 2):
                    dr = dr + (ur[b] * re[b] - ui[b] * im[b])
                    di = di + (ur[b] * im[b] + ui[b] * re[b])
                store(0, a, m, lanes, dr.astype(jnp.bfloat16))
                store(1, a, m, lanes, di.astype(jnp.bfloat16))
            return carry

        lax.fori_loop(0, count // ROWS, body, 0, unroll=2)


def rows_by_own(slabs, own):
    return slabs % 4 == 0 and own % 8 == 0


def inner(left, right):
    return lax.dot_general(left, right, (((1,), (1,)), ((), ())), preferred_element_type=jnp.float32)


def finish(sum_re, sum_im, slabs, core, order, acc, send, keep):
    count = send.shape[0]
    own = count // slabs
    acc[0] = sum_re - sum_re.T
    acc[1] = sum_im + sum_im.T
    if not rows_by_own(slabs, own):
        send[...] = acc[1 - core].astype(jnp.bfloat16)
        keep[...] = acc[core]
        return
    for k in range(slabs // 2):
        block = slice(k * 2 * own, (k + 1) * 2 * own)

        def rows(which):
            at = pl.ds(pl.multiple_of((2 * order[k] + which) * own, 8), own)
            return jnp.concatenate([acc[0, at, :], acc[1, at, :]], axis=0)

        send[block, :] = rows(1 - core).astype(jnp.bfloat16)
        keep[block, :] = rows(core)


def x_kernel(slabs, where_ref, field_ref, links_ref, send, keep, right, acc):
    count = field_ref.shape[1]

    def store(part, a, m, lanes, value):
        right[a, pl.ds(pl.multiple_of(part * count + m * ROWS, ROWS), ROWS), lanes] = value

    times_links(field_ref, links_ref, 0, False, True, store)
    product = [None, None]
    for b in range(3):
        for part in range(2):
            term = inner(field_ref[part * 3 + b], right[b])
            product[part] = term if b == 0 else product[part] + term
    sum_re = product[0][:, :count] + product[1][:, count:]
    sum_im = product[0][:, count:] - product[1][:, :count]
    finish(sum_re, sum_im, slabs, where_ref[0], range(slabs // 2), acc, send, keep)


def w_kernel(field_ref, links_ref, keep_ref, got_ref, w_ref, chip_ref):
    chip_ref[...] = (keep_ref[...] + got_ref[...].astype(jnp.float32)).astype(jnp.bfloat16)

    def store(part, a, m, lanes, value):
        w_ref[part * 3 + a, pl.ds(pl.multiple_of(m * ROWS, ROWS), ROWS), lanes] = value

    times_links(field_ref, links_ref, 1, True, False, store)


def z_order(chip, chips):
    along = chips // 2
    ahead = [lax.rem((chip >> 1) + r, along) * 2 for r in range(along)]
    low = chip & 1
    return [to + 1 - low for to in ahead] + [to + low for to in ahead]


def z_kernel(slabs, where_ref, w_hbm, face_hbm, send, keep, left, right, acc, sems):
    count = w_hbm.shape[1]
    copies = []
    for b in range(3):
        group = []
        for part in range(2):
            k = part * 3 + b
            rows = pl.ds(part * count, count)
            group.append(pltpu.make_async_copy(face_hbm.at[k], right.at[b, rows], sems.at[k]))
            group.append(pltpu.make_async_copy(w_hbm.at[k], left.at[k], sems.at[6 + k]))
        for copy in group:
            copy.start()
        copies.append(group)
    product = [None, None]
    for b in range(3):
        for copy in copies[b]:
            copy.wait()
        for part in range(2):
            term = inner(left[part * 3 + b], right[b])
            product[part] = term if b == 0 else product[part] + term
    sum_re = product[0][:, :count] + product[1][:, count:]
    sum_im = product[0][:, count:] - product[1][:, :count]
    finish(sum_re, sum_im, slabs, where_ref[0], z_order(where_ref[1], slabs // 2), acc, send, keep)


def call(body, outs, specs, scratch, mib, flops, moved):
    return pl.pallas_call(
        body,
        out_shape=outs,
        in_specs=specs,
        out_specs=[VMEM] * len(outs),
        scratch_shapes=scratch,
        compiler_params=pltpu.CompilerParams(vmem_limit_bytes=mib * 2**20),
        cost_estimate=pl.CostEstimate(flops=flops, bytes_accessed=moved, transcendentals=0),
    )


def shards(vectors, links):
    slabs = lax.axis_size("gz")
    count, planes, sites = vectors.shape[1], vectors.shape[3], vectors.shape[4]
    assert planes == 1 and slabs % 2 == 0
    own = count // slabs
    scale = 1.0 / math.sqrt(12.0 * sites * planes * slabs)
    index = lax.axis_index("gz").astype(jnp.int32)
    where = jnp.stack([index & 1, index >> 1])
    field = jnp.transpose(vectors, (0, 2, 3, 1, 4)).reshape(6, count, sites)
    links = links.reshape(36, sites)
    face = passed_along(field, "gz", -1)

    flops = 24 * count * count * sites
    moved = 12 * count * sites
    halves = [
        jax.ShapeDtypeStruct((count, count), jnp.bfloat16),
        jax.ShapeDtypeStruct((count, count), jnp.float32),
    ]
    stacked = pltpu.VMEM((3, 2 * count, sites), jnp.bfloat16)
    square = pltpu.VMEM((2, count, count), jnp.float32)
    send_x, keep_x = call(
        functools.partial(x_kernel, slabs), halves, [SMEM, VMEM, VMEM],
        [stacked, square], 22, flops, moved,
    )(where, field, links)
    w, chip_x = call(
        w_kernel, [jax.ShapeDtypeStruct(field.shape, jnp.bfloat16), halves[0]], [VMEM] * 4, [], 12,
        count * sites * 66, 2 * moved,
    )(field, links, keep_x, swapped(send_x, "gz"))

    if rows_by_own(slabs, own):
        groups = [list(range(c, slabs, 2)) for c in range(2)]
        blocks = (slabs // 2, 1, 2 * own, count)
    else:
        groups = None
        blocks = (slabs // 2, 2, own, count)

    def exchanged(chip):
        chip = chip.reshape((-1,) + blocks[2:])
        return lax.all_to_all(chip, "gz", 0, 0, axis_index_groups=groups)

    def total(got):
        return jnp.sum(got.reshape(blocks).astype(jnp.float32), axis=0).reshape(2, own, count)

    got_x = exchanged(chip_x)
    send_z, keep_z = call(
        functools.partial(z_kernel, slabs), halves, [SMEM, ANY, ANY],
        [
            pltpu.VMEM(field.shape, jnp.bfloat16), stacked, square, pltpu.SemaphoreType.DMA((12,)),
        ],
        58, flops, moved,
    )(where, w, face)
    send_z, got_x = lax.optimization_barrier((send_z, got_x))
    chip_z = keep_z + swapped(send_z, "gz").astype(jnp.float32)
    if rows_by_own(slabs, own):
        half = count // 2
        other = chip_z[:half].astype(jnp.bfloat16)
        near = lax.ppermute(other, "gz", [(i, i ^ 2) for i in range(slabs)])
        line = chip_z[half:] + near.astype(jnp.float32)
        total_z = line[: 2 * own]
        for r in range(1, slabs // 4):
            block = line[r * 2 * own : (r + 1) * 2 * own].astype(jnp.bfloat16)
            total_z = total_z + passed_along(block, "gz", 4 * r).astype(jnp.float32)
        total_z = total_z.reshape(2, own, count)
    else:
        total_z = total(exchanged(chip_z.astype(jnp.bfloat16)))
    both = jnp.concatenate([total(got_x), total_z], axis=0)
    return jnp.transpose(both, (1, 0, 2)) * scale


def solution(mesh):
    return jax.shard_map(
        shards,
        mesh=mesh,
        in_specs=(P("grp", None, None, "gz", None), P("grp", None, None, None, "gz", None)),
        out_specs=P("gz", "grp", None),
        check_vma=False,
    )
```

```python
import functools
import math

import jax
import jax.numpy as jnp
from jax import lax
from jax.experimental import pallas as pl
from jax.experimental.pallas import tpu as pltpu
from jax.sharding import PartitionSpec as P

X = 64
LANES = 128
ROWS = 16
VMEM = pl.BlockSpec(memory_space=pltpu.VMEM)
SMEM = pl.BlockSpec(memory_space=pltpu.SMEM)
ANY = pl.BlockSpec(memory_space=pl.ANY)


def passed_along(block, axis, distance):
    devices = range(lax.axis_size(axis))
    route = [((i - distance) % len(devices), i) for i in devices]
    return lax.ppermute(block, axis, route)


def swapped(block, axis):
    return lax.ppermute(block, axis, [(i, i ^ 1) for i in range(lax.axis_size(axis))])


def times_links(field_ref, links_ref, mu, adjoint, roll, store):
    count, sites = field_ref.shape[1:]
    for t in range(sites // LANES):
        lanes = slice(t * LANES, (t + 1) * LANES)

        def link(part, a, b):
            row = ((part * 2 + mu) * 3 + a) * 3 + b
            value = jnp.broadcast_to(links_ref[row : row + 1, lanes], (ROWS, LANES))
            return -value if adjoint and part == 1 else value

        def links_of(part, a):
            return [link(part, b, a) if adjoint else link(part, a, b) for b in range(3)]

        u = [[links_of(p, a) for a in range(3)] for p in range(2)]
        if roll:
            lane = lax.broadcasted_iota(jnp.int32, (ROWS, LANES), 1)
            last = (lane & (X - 1)) == X - 1

        def body(m, carry):
            rows = pl.ds(pl.multiple_of(m * ROWS, ROWS), ROWS)
            v = []
            for k in range(6):
                value = field_ref[k, rows, lanes].astype(jnp.float32)
                if roll:
                    ahead = pltpu.roll(value, LANES - 1, 1)
                    around = pltpu.roll(value, X - 1, 1)
                    value = jnp.where(last, around, ahead)
                v.append(value)
            re, im = v[:3], v[3:]
            for a in range(3):
                ur, ui = u[0][a], u[1][a]
                dr = ur[0] * re[0] - ui[0] * im[0]
                di = ur[0] * im[0] + ui[0] * re[0]
                for b in (1, 2):
                    dr = dr + (ur[b] * re[b] - ui[b] * im[b])
                    di = di + (ur[b] * im[b] + ui[b] * re[b])
                store(0, a, m, lanes, dr.astype(jnp.bfloat16))
                store(1, a, m, lanes, di.astype(jnp.bfloat16))
            return carry

        lax.fori_loop(0, count // ROWS, body, 0, unroll=2)


def rows_by_own(slabs, own):
    return slabs % 4 == 0 and own % 8 == 0


def inner(left, right):
    return lax.dot_general(left, right, (((1,), (1,)), ((), ())), preferred_element_type=jnp.float32)


def finish(sum_re, sum_im, slabs, core, order, acc, send, keep):
    count = send.shape[0]
    own = count // slabs
    acc[0] = sum_re - sum_re.T
    acc[1] = sum_im + sum_im.T
    if not rows_by_own(slabs, own):
        send[...] = acc[1 - core].astype(jnp.bfloat16)
        keep[...] = acc[core]
        return
    for k in range(slabs // 2):
        block = slice(k * 2 * own, (k + 1) * 2 * own)

        def rows(which):
            at = pl.ds(pl.multiple_of((2 * order[k] + which) * own, 8), own)
            return jnp.concatenate([acc[0, at, :], acc[1, at, :]], axis=0)

        send[block, :] = rows(1 - core).astype(jnp.bfloat16)
        keep[block, :] = rows(core)


def x_kernel(slabs, where_ref, field_ref, links_ref, send, keep, right, acc):
    count = field_ref.shape[1]

    def store(part, a, m, lanes, value):
        right[a, pl.ds(pl.multiple_of(part * count + m * ROWS, ROWS), ROWS), lanes] = value

    times_links(field_ref, links_ref, 0, False, True, store)
    product = [None, None]
    for b in range(3):
        for part in range(2):
            term = inner(field_ref[part * 3 + b], right[b])
            product[part] = term if b == 0 else product[part] + term
    sum_re = product[0][:, :count] + product[1][:, count:]
    sum_im = product[0][:, count:] - product[1][:, :count]
    finish(sum_re, sum_im, slabs, where_ref[0], range(slabs // 2), acc, send, keep)


def w_kernel(field_ref, links_ref, after_ref, w_ref):
    def store(part, a, m, lanes, value):
        w_ref[part * 3 + a, pl.ds(pl.multiple_of(m * ROWS, ROWS), ROWS), lanes] = value

    times_links(field_ref, links_ref, 1, True, False, store)


def z_order(chip, chips):
    along = chips // 2
    ahead = [lax.rem((chip >> 1) + r, along) * 2 for r in range(along)]
    low = chip & 1
    return [to + 1 - low for to in ahead] + [to + low for to in ahead]


def z_kernel(slabs, where_ref, w_ref, face_hbm, send, keep, right, acc, sems):
    count = w_ref.shape[1]
    copies = []
    for b in range(3):
        group = []
        for part in range(2):
            k = part * 3 + b
            rows = pl.ds(part * count, count)
            group.append(pltpu.make_async_copy(face_hbm.at[k], right.at[b, rows], sems.at[k]))
        for copy in group:
            copy.start()
        copies.append(group)
    product = [None, None]
    for b in range(3):
        for copy in copies[b]:
            copy.wait()
        for part in range(2):
            term = inner(w_ref[part * 3 + b], right[b])
            product[part] = term if b == 0 else product[part] + term
    sum_re = product[0][:, :count] + product[1][:, count:]
    sum_im = product[0][:, count:] - product[1][:, :count]
    finish(sum_re, sum_im, slabs, where_ref[0], z_order(where_ref[1], slabs // 2), acc, send, keep)


def call(body, outs, specs, scratch, mib, flops, moved):
    return pl.pallas_call(
        body,
        out_shape=outs,
        in_specs=specs,
        out_specs=[VMEM] * len(outs),
        scratch_shapes=scratch,
        compiler_params=pltpu.CompilerParams(vmem_limit_bytes=mib * 2**20),
        cost_estimate=pl.CostEstimate(flops=flops, bytes_accessed=moved, transcendentals=0),
    )


def shards(vectors, links):
    slabs = lax.axis_size("gz")
    count, planes, sites = vectors.shape[1], vectors.shape[3], vectors.shape[4]
    assert planes == 1 and slabs % 2 == 0
    own = count // slabs
    scale = 1.0 / math.sqrt(12.0 * sites * planes * slabs)
    index = lax.axis_index("gz").astype(jnp.int32)
    where = jnp.stack([index & 1, index >> 1])
    field = jnp.transpose(vectors, (0, 2, 3, 1, 4)).reshape(6, count, sites)
    links = links.reshape(36, sites)
    face = passed_along(field, "gz", -1)

    flops = 24 * count * count * sites
    moved = 12 * count * sites
    halves = [
        jax.ShapeDtypeStruct((count, count), jnp.bfloat16),
        jax.ShapeDtypeStruct((count, count), jnp.float32),
    ]
    stacked = pltpu.VMEM((3, 2 * count, sites), jnp.bfloat16)
    square = pltpu.VMEM((2, count, count), jnp.float32)
    send_x, keep_x = call(
        functools.partial(x_kernel, slabs), halves, [SMEM, VMEM, VMEM],
        [stacked, square], 16, flops, moved,
    )(where, field, links)
    chip_x = (keep_x + swapped(send_x, "gz").astype(jnp.float32)).astype(jnp.bfloat16)
    (w,) = call(
        w_kernel, [jax.ShapeDtypeStruct(field.shape, jnp.bfloat16)], [VMEM, VMEM, ANY], [], 10,
        count * sites * 66, 2 * moved,
    )(field, links, chip_x)

    if rows_by_own(slabs, own):
        groups = [list(range(c, slabs, 2)) for c in range(2)]
        blocks = (slabs // 2, 1, 2 * own, count)
    else:
        groups = None
        blocks = (slabs // 2, 2, own, count)

    def exchanged(chip):
        chip = chip.reshape((-1,) + blocks[2:])
        return lax.all_to_all(chip, "gz", 0, 0, axis_index_groups=groups)

    def total(got):
        return jnp.sum(got.reshape(blocks).astype(jnp.float32), axis=0).reshape(2, own, count)

    got_x = exchanged(chip_x)
    send_z, keep_z = call(
        functools.partial(z_kernel, slabs), halves, [SMEM, VMEM, ANY],
        [stacked, square, pltpu.SemaphoreType.DMA((6,))], 14, flops, moved,
    )(where, w, face)
    send_z, got_x = lax.optimization_barrier((send_z, got_x))
    chip_z = keep_z + swapped(send_z, "gz").astype(jnp.float32)
    if rows_by_own(slabs, own):
        half = count // 2
        other = chip_z[:half].astype(jnp.bfloat16)
        near = lax.ppermute(other, "gz", [(i, i ^ 2) for i in range(slabs)])
        line = chip_z[half:] + near.astype(jnp.float32)
        total_z = line[: 2 * own]
        for r in range(1, slabs // 4):
            block = line[r * 2 * own : (r + 1) * 2 * own].astype(jnp.bfloat16)
            total_z = total_z + passed_along(block, "gz", 4 * r).astype(jnp.float32)
        total_z = total_z.reshape(2, own, count)
    else:
        total_z = total(exchanged(chip_z.astype(jnp.bfloat16)))
    both = jnp.concatenate([total(got_x), total_z], axis=0)
    return jnp.transpose(both, (1, 0, 2)) * scale


def solution(mesh):
    return jax.shard_map(
        shards,
        mesh=mesh,
        in_specs=(P("grp", None, None, "gz", None), P("grp", None, None, None, "gz", None)),
        out_specs=P("gz", "grp", None),
        check_vma=False,
    )
```

```python
import functools
import math

import jax
import jax.numpy as jnp
from jax import lax
from jax.experimental import pallas as pl
from jax.experimental.pallas import tpu as pltpu
from jax.sharding import PartitionSpec as P

X = 64
LANES = 128
ROWS = 16
VMEM = pl.BlockSpec(memory_space=pltpu.VMEM)
SMEM = pl.BlockSpec(memory_space=pltpu.SMEM)
ANY = pl.BlockSpec(memory_space=pl.ANY)


def passed_along(block, axis, distance):
    devices = range(lax.axis_size(axis))
    route = [((i - distance) % len(devices), i) for i in devices]
    return lax.ppermute(block, axis, route)


def swapped(block, axis):
    return lax.ppermute(block, axis, [(i, i ^ 1) for i in range(lax.axis_size(axis))])


def times_links(field_ref, links_ref, mu, adjoint, roll, store):
    count, sites = field_ref.shape[1:]
    for t in range(sites // LANES):
        lanes = slice(t * LANES, (t + 1) * LANES)

        def link(part, a, b):
            row = ((part * 2 + mu) * 3 + a) * 3 + b
            value = jnp.broadcast_to(links_ref[row : row + 1, lanes], (ROWS, LANES))
            return -value if adjoint and part == 1 else value

        def links_of(part, a):
            return [link(part, b, a) if adjoint else link(part, a, b) for b in range(3)]

        u = [[links_of(p, a) for a in range(3)] for p in range(2)]
        if roll:
            lane = lax.broadcasted_iota(jnp.int32, (ROWS, LANES), 1)
            last = (lane & (X - 1)) == X - 1

        def body(m, carry):
            rows = pl.ds(pl.multiple_of(m * ROWS, ROWS), ROWS)
            v = []
            for k in range(6):
                value = field_ref[k, rows, lanes].astype(jnp.float32)
                if roll:
                    ahead = pltpu.roll(value, LANES - 1, 1)
                    around = pltpu.roll(value, X - 1, 1)
                    value = jnp.where(last, around, ahead)
                v.append(value)
            re, im = v[:3], v[3:]
            for a in range(3):
                ur, ui = u[0][a], u[1][a]
                dr = ur[0] * re[0] - ui[0] * im[0]
                di = ur[0] * im[0] + ui[0] * re[0]
                for b in (1, 2):
                    dr = dr + (ur[b] * re[b] - ui[b] * im[b])
                    di = di + (ur[b] * im[b] + ui[b] * re[b])
                store(0, a, m, lanes, dr.astype(jnp.bfloat16))
                store(1, a, m, lanes, di.astype(jnp.bfloat16))
            return carry

        lax.fori_loop(0, count // ROWS, body, 0, unroll=2)


def rows_by_own(slabs, own):
    return slabs % 4 == 0 and own % 8 == 0


def inner(left, right):
    return lax.dot_general(left, right, (((1,), (1,)), ((), ())), preferred_element_type=jnp.float32)


def block_order(chip, chips):
    along = chips // 2
    ahead = [lax.rem((chip >> 1) + r, along) * 2 for r in range(along)]
    low = chip & 1
    return [to + 1 - low for to in ahead] + [to + low for to in ahead]


def finish(sum_re, sum_im, slabs, core, order, acc, send, keep):
    count = send.shape[0]
    own = count // slabs
    acc[0] = sum_re - sum_re.T
    acc[1] = sum_im + sum_im.T
    if not rows_by_own(slabs, own):
        send[...] = acc[1 - core].astype(jnp.bfloat16)
        keep[...] = acc[core]
        return
    for k in range(slabs // 2):
        block = slice(k * 2 * own, (k + 1) * 2 * own)

        def rows(which):
            at = pl.ds(pl.multiple_of((2 * order[k] + which) * own, 8), own)
            return jnp.concatenate([acc[0, at, :], acc[1, at, :]], axis=0)

        send[block, :] = rows(1 - core).astype(jnp.bfloat16)
        keep[block, :] = rows(core)


def x_kernel(slabs, where_ref, field_ref, links_ref, send, keep, right, acc):
    count = field_ref.shape[1]

    def store(part, a, m, lanes, value):
        right[a, pl.ds(pl.multiple_of(part * count + m * ROWS, ROWS), ROWS), lanes] = value

    times_links(field_ref, links_ref, 0, False, True, store)
    product = [None, None]
    for b in range(3):
        for part in range(2):
            term = inner(field_ref[part * 3 + b], right[b])
            product[part] = term if b == 0 else product[part] + term
    sum_re = product[0][:, :count] + product[1][:, count:]
    sum_im = product[0][:, count:] - product[1][:, :count]
    finish(sum_re, sum_im, slabs, where_ref[0], block_order(where_ref[1], slabs // 2), acc, send, keep)


def w_kernel(field_ref, links_ref, w_ref):
    def store(part, a, m, lanes, value):
        w_ref[part * 3 + a, pl.ds(pl.multiple_of(m * ROWS, ROWS), ROWS), lanes] = value

    times_links(field_ref, links_ref, 1, True, False, store)


def z_kernel(slabs, where_ref, w_ref, face_hbm, send, keep, right, acc, sems):
    count = w_ref.shape[1]
    copies = []
    for b in range(3):
        group = []
        for part in range(2):
            k = part * 3 + b
            rows = pl.ds(part * count, count)
            group.append(pltpu.make_async_copy(face_hbm.at[k], right.at[b, rows], sems.at[k]))
        for copy in group:
            copy.start()
        copies.append(group)
    product = [None, None]
    for b in range(3):
        for copy in copies[b]:
            copy.wait()
        for part in range(2):
            term = inner(w_ref[part * 3 + b], right[b])
            product[part] = term if b == 0 else product[part] + term
    sum_re = product[0][:, :count] + product[1][:, count:]
    sum_im = product[0][:, count:] - product[1][:, :count]
    finish(sum_re, sum_im, slabs, where_ref[0], block_order(where_ref[1], slabs // 2), acc, send, keep)


def call(body, outs, specs, scratch, mib, flops, moved):
    return pl.pallas_call(
        body,
        out_shape=outs,
        in_specs=specs,
        out_specs=[VMEM] * len(outs),
        scratch_shapes=scratch,
        compiler_params=pltpu.CompilerParams(vmem_limit_bytes=mib * 2**20),
        cost_estimate=pl.CostEstimate(flops=flops, bytes_accessed=moved, transcendentals=0),
    )


def shards(vectors, links):
    slabs = lax.axis_size("gz")
    count, planes, sites = vectors.shape[1], vectors.shape[3], vectors.shape[4]
    assert planes == 1 and slabs % 2 == 0
    own = count // slabs
    scale = 1.0 / math.sqrt(12.0 * sites * planes * slabs)
    index = lax.axis_index("gz").astype(jnp.int32)
    where = jnp.stack([index & 1, index >> 1])
    field = jnp.transpose(vectors, (0, 2, 3, 1, 4)).reshape(6, count, sites)
    links = links.reshape(36, sites)
    face = passed_along(field, "gz", -1)

    flops = 24 * count * count * sites
    moved = 12 * count * sites
    halves = [
        jax.ShapeDtypeStruct((count, count), jnp.bfloat16),
        jax.ShapeDtypeStruct((count, count), jnp.float32),
    ]
    stacked = pltpu.VMEM((3, 2 * count, sites), jnp.bfloat16)
    square = pltpu.VMEM((2, count, count), jnp.float32)
    send_x, keep_x = call(
        functools.partial(x_kernel, slabs), halves, [SMEM, VMEM, VMEM],
        [stacked, square], 16, flops, moved,
    )(where, field, links)
    (w,) = call(
        w_kernel, [jax.ShapeDtypeStruct(field.shape, jnp.bfloat16)], [VMEM, VMEM], [], 10,
        count * sites * 66, 2 * moved,
    )(field, links)
    chip_x = keep_x + swapped(send_x, "gz").astype(jnp.float32)
    other_x = chip_x[: count // 2].astype(jnp.bfloat16)
    face, other_x = lax.optimization_barrier((face, other_x))

    def from_neighbour(other):
        return lax.ppermute(other, "gz", [(i, i ^ 2) for i in range(slabs)]).astype(jnp.float32)

    def total(line):
        result = line[: 2 * own]
        for r in range(1, slabs // 4):
            block = line[r * 2 * own : (r + 1) * 2 * own].astype(jnp.bfloat16)
            result = result + passed_along(block, "gz", 4 * r).astype(jnp.float32)
        return result.reshape(2, own, count)

    def exchanged(chip):
        chip = chip.astype(jnp.bfloat16).reshape(slabs, own, count)
        got = lax.all_to_all(chip, "gz", 0, 0).reshape(slabs // 2, 2, own, count)
        return jnp.sum(got.astype(jnp.float32), axis=0)

    near_x = from_neighbour(other_x) if rows_by_own(slabs, own) else None
    send_z, keep_z = call(
        functools.partial(z_kernel, slabs), halves, [SMEM, VMEM, ANY],
        [stacked, square, pltpu.SemaphoreType.DMA((6,))], 14, flops, moved,
    )(where, w, face)
    chip_z = keep_z + swapped(send_z, "gz").astype(jnp.float32)
    if rows_by_own(slabs, own):
        half = count // 2
        near_z = from_neighbour(chip_z[:half].astype(jnp.bfloat16))
        totals = [total(chip_x[half:] + near_x), total(chip_z[half:] + near_z)]
    else:
        totals = [exchanged(chip_x), exchanged(chip_z)]
    both = jnp.concatenate(totals, axis=0)
    return jnp.transpose(both, (1, 0, 2)) * scale


def solution(mesh):
    return jax.shard_map(
        shards,
        mesh=mesh,
        in_specs=(P("grp", None, None, "gz", None), P("grp", None, None, None, "gz", None)),
        out_specs=P("gz", "grp", None),
        check_vma=False,
    )
```

```python
import functools
import math

import jax
import jax.numpy as jnp
from jax import lax
from jax.experimental import pallas as pl
from jax.experimental.pallas import tpu as pltpu
from jax.sharding import PartitionSpec as P

X = 64
LANES = 128
ROWS = 16
VMEM = pl.BlockSpec(memory_space=pltpu.VMEM)
SMEM = pl.BlockSpec(memory_space=pltpu.SMEM)
ANY = pl.BlockSpec(memory_space=pl.ANY)


def passed_along(block, axis, distance):
    devices = range(lax.axis_size(axis))
    route = [((i - distance) % len(devices), i) for i in devices]
    return lax.ppermute(block, axis, route)


def swapped(block, axis):
    return lax.ppermute(block, axis, [(i, i ^ 1) for i in range(lax.axis_size(axis))])


def times_links(field_ref, coef_ref, roll, store):
    count, sites = field_ref.shape[1:]
    for t in range(sites // LANES):
        lanes = slice(t * LANES, (t + 1) * LANES)

        def coef(part, a, b):
            row = (part * 3 + a) * 3 + b
            return jnp.broadcast_to(coef_ref[row : row + 1, lanes], (ROWS, LANES))

        u = [[[coef(p, a, b) for b in range(3)] for a in range(3)] for p in range(2)]
        if roll:
            lane = lax.broadcasted_iota(jnp.int32, (ROWS, LANES), 1)
            last = (lane & (X - 1)) == X - 1

        def body(m, carry):
            rows = pl.ds(pl.multiple_of(m * ROWS, ROWS), ROWS)
            v = []
            for k in range(6):
                value = field_ref[k, rows, lanes].astype(jnp.float32)
                if roll:
                    ahead = pltpu.roll(value, LANES - 1, 1)
                    around = pltpu.roll(value, X - 1, 1)
                    value = jnp.where(last, around, ahead)
                v.append(value)
            re, im = v[:3], v[3:]
            for a in range(3):
                ur, ui = u[0][a], u[1][a]
                dr = ur[0] * re[0] - ui[0] * im[0]
                di = ur[0] * im[0] + ui[0] * re[0]
                for b in (1, 2):
                    dr = dr + (ur[b] * re[b] - ui[b] * im[b])
                    di = di + (ur[b] * im[b] + ui[b] * re[b])
                store(0, a, m, lanes, dr.astype(jnp.bfloat16))
                store(1, a, m, lanes, di.astype(jnp.bfloat16))
            return carry

        lax.fori_loop(0, count // ROWS, body, 0, unroll=2)


def rows_by_own(slabs, own):
    return slabs % 4 == 0 and own % 8 == 0


def inner(left, right):
    return lax.dot_general(left, right, (((1,), (1,)), ((), ())), preferred_element_type=jnp.float32)


def finish(sum_re, sum_im, slabs, core, order, acc, send, keep):
    count = send.shape[0]
    own = count // slabs
    acc[0] = sum_re - sum_re.T
    acc[1] = sum_im + sum_im.T
    if not rows_by_own(slabs, own):
        send[...] = acc[1 - core].astype(jnp.bfloat16)
        keep[...] = acc[core]
        return
    for k in range(slabs // 2):
        block = slice(k * 2 * own, (k + 1) * 2 * own)

        def rows(which):
            at = pl.ds(pl.multiple_of((2 * order[k] + which) * own, 8), own)
            return jnp.concatenate([acc[0, at, :], acc[1, at, :]], axis=0)

        send[block, :] = rows(1 - core).astype(jnp.bfloat16)
        keep[block, :] = rows(core)


def x_kernel(slabs, where_ref, field_ref, links_ref, send, keep, right, acc):
    count = field_ref.shape[1]

    def store(part, a, m, lanes, value):
        right[a, pl.ds(pl.multiple_of(part * count + m * ROWS, ROWS), ROWS), lanes] = value

    times_links(field_ref, links_ref, True, store)
    product = [None, None]
    for b in range(3):
        for part in range(2):
            term = inner(field_ref[part * 3 + b], right[b])
            product[part] = term if b == 0 else product[part] + term
    sum_re = product[0][:, :count] + product[1][:, count:]
    sum_im = product[0][:, count:] - product[1][:, :count]
    finish(sum_re, sum_im, slabs, where_ref[0], range(slabs // 2), acc, send, keep)


def cut_kernel(where_ref, field_hbm, half_hbm, sems):
    half = half_hbm.shape[2]
    lanes = pl.ds(pl.multiple_of(where_ref[0] * half, LANES), half)
    copies = [
        pltpu.make_async_copy(field_hbm.at[k, :, lanes], half_hbm.at[k], sems.at[k])
        for k in range(field_hbm.shape[0])
    ]
    for copy in copies:
        copy.start()
    for copy in copies:
        copy.wait()


def b_kernel(field_ref, coef_ref, after_ref, b_ref):
    count, sites = field_ref.shape[1:]
    half = sites // 2

    def store(part, a, m, lanes, value):
        rows = pl.ds(pl.multiple_of(part * count + m * ROWS, ROWS), ROWS)
        start = a * half + lanes.start % half
        b_ref[lanes.start // half, rows, start : start + LANES] = value

    times_links(field_ref, coef_ref, False, store)


def z_order(chip, chips):
    along = chips // 2
    ahead = [lax.rem((chip >> 1) + r, along) * 2 for r in range(along)]
    low = chip & 1
    return [to + 1 - low for to in ahead] + [to + low for to in ahead]


def z_kernel(near, slabs, where_ref, b_ref, got_hbm, *refs):
    if near:
        out, right, sems = refs
    else:
        before, send, keep, right, acc, sems = refs
    count, half = got_hbm.shape[1], right.shape[1] // 3
    core = where_ref[0]
    which = core if near else 1 - core
    lanes = pl.ds(pl.multiple_of(which * half, LANES), half) if near else pl.ds(0, half)
    copies = []
    for part in range(2):
        for b in range(3):
            k = part * 3 + b
            to = right.at[pl.ds(part * count, count), pl.ds(b * half, half)]
            copies.append(pltpu.make_async_copy(got_hbm.at[k, :, lanes], to, sems.at[k]))
    for copy in copies:
        copy.start()
    for copy in copies:
        copy.wait()
    sign = (1 - 2 * which).astype(jnp.float32)
    from_re = inner(b_ref[which, :count, :], right[...])
    from_im = inner(b_ref[which, count:, :], right[...])
    sum_re = (from_re[:, :count] + from_im[:, count:]) * sign
    sum_im = (from_re[:, count:] - from_im[:, :count]) * sign
    if near:
        out[0] = sum_re
        out[1] = sum_im
    else:
        order = z_order(where_ref[1], slabs // 2)
        finish(before[0] + sum_re, before[1] + sum_im, slabs, core, order, acc, send, keep)


def call(body, outs, specs, scratch, mib, flops, moved, where=VMEM):
    return pl.pallas_call(
        body,
        out_shape=outs,
        in_specs=specs,
        out_specs=[where] * len(outs),
        scratch_shapes=scratch,
        compiler_params=pltpu.CompilerParams(vmem_limit_bytes=mib * 2**20),
        cost_estimate=pl.CostEstimate(flops=flops, bytes_accessed=moved, transcendentals=0),
    )


def shards(vectors, links):
    slabs = lax.axis_size("gz")
    count, planes, sites = vectors.shape[1], vectors.shape[3], vectors.shape[4]
    assert planes == 1 and slabs % 2 == 0
    own = count // slabs
    scale = 1.0 / math.sqrt(12.0 * sites * planes * slabs)
    index = lax.axis_index("gz").astype(jnp.int32)
    where = jnp.stack([index & 1, index >> 1])
    field = jnp.transpose(vectors, (0, 2, 3, 1, 4)).reshape(6, count, sites)
    half = sites // 2
    (cut,) = call(
        cut_kernel, [jax.ShapeDtypeStruct((6, count, half), vectors.dtype)], [SMEM, ANY],
        [pltpu.SemaphoreType.DMA((6,))], 60, 0, 12 * count * half, ANY,
    )(where, field)
    far = lax.ppermute(cut, "gz", [(i, (i + i % 2 * 2 - 1) % slabs) for i in range(slabs)])
    near = swapped(field, "gz")
    links = links.reshape(2, 2, 3, 3, sites)
    links_x, links_z = links[:, 0].reshape(18, sites), links[:, 1]
    conjugate = jnp.array([1.0, -1.0], jnp.float32).reshape(2, 1, 1, 1)
    adjoint = jnp.transpose(links_z[..., :half], (0, 2, 1, 3)) * conjugate
    coefs = jnp.concatenate([adjoint, passed_along(links_z[..., half:], "gz", 1)], axis=-1)
    coefs = coefs.reshape(18, sites)

    flops = 24 * count * count * sites
    moved = 12 * count * sites
    halves = [
        jax.ShapeDtypeStruct((count, count), jnp.bfloat16),
        jax.ShapeDtypeStruct((count, count), jnp.float32),
    ]
    stacked = pltpu.VMEM((3, 2 * count, sites), jnp.bfloat16)
    square = pltpu.VMEM((2, count, count), jnp.float32)
    send_x, keep_x = call(
        functools.partial(x_kernel, slabs), halves, [SMEM, VMEM, VMEM],
        [stacked, square], 16, flops, moved,
    )(where, field, links_x)
    chip_x = (keep_x + swapped(send_x, "gz").astype(jnp.float32)).astype(jnp.bfloat16)
    (prepared,) = call(
        b_kernel, [jax.ShapeDtypeStruct((2, 2 * count, 3 * half), jnp.bfloat16)], [VMEM, VMEM, ANY],
        [], 10, count * sites * 66, 2 * moved,
    )(field, coefs, chip_x)
    right = [pltpu.VMEM((2 * count, 3 * half), jnp.bfloat16)]
    sems = [pltpu.SemaphoreType.DMA((6,))]
    (first,) = call(
        functools.partial(z_kernel, True, slabs), [jax.ShapeDtypeStruct((2, count, count), jnp.float32)],
        [SMEM, VMEM, ANY], right + sems, 14, flops // 2, moved // 2,
    )(where, prepared, near)

    if rows_by_own(slabs, own):
        groups = [list(range(c, slabs, 2)) for c in range(2)]
        blocks = (slabs // 2, 1, 2 * own, count)
    else:
        groups = None
        blocks = (slabs // 2, 2, own, count)

    def exchanged(chip):
        chip = chip.reshape((-1,) + blocks[2:])
        return lax.all_to_all(chip, "gz", 0, 0, axis_index_groups=groups)

    def total(got):
        return jnp.sum(got.reshape(blocks).astype(jnp.float32), axis=0).reshape(2, own, count)

    got_x = exchanged(chip_x)
    send_z, keep_z = call(
        functools.partial(z_kernel, False, slabs), halves, [SMEM, VMEM, ANY, VMEM],
        right + [square] + sems, 14, flops // 2, moved // 2,
    )(where, prepared, far, first)
    send_z, got_x = lax.optimization_barrier((send_z, got_x))
    chip_z = keep_z + swapped(send_z, "gz").astype(jnp.float32)
    if rows_by_own(slabs, own):
        rows = count // 2
        other = chip_z[:rows].astype(jnp.bfloat16)
        near = lax.ppermute(other, "gz", [(i, i ^ 2) for i in range(slabs)])
        line = chip_z[rows:] + near.astype(jnp.float32)
        total_z = line[: 2 * own]
        for r in range(1, slabs // 4):
            block = line[r * 2 * own : (r + 1) * 2 * own].astype(jnp.bfloat16)
            total_z = total_z + passed_along(block, "gz", 4 * r).astype(jnp.float32)
        total_z = total_z.reshape(2, own, count)
    else:
        total_z = total(exchanged(chip_z.astype(jnp.bfloat16)))
    both = jnp.concatenate([total(got_x), total_z], axis=0)
    return jnp.transpose(both, (1, 0, 2)) * scale


def solution(mesh):
    return jax.shard_map(
        shards,
        mesh=mesh,
        in_specs=(P("grp", None, None, "gz", None), P("grp", None, None, None, "gz", None)),
        out_specs=P("gz", "grp", None),
        check_vma=False,
    )
```

```python
import functools
import math

import jax
import jax.numpy as jnp
from jax import lax
from jax.experimental import pallas as pl
from jax.experimental.pallas import tpu as pltpu
from jax.sharding import PartitionSpec as P

X = 64
LANES = 128
ROWS = 16
VMEM = pl.BlockSpec(memory_space=pltpu.VMEM)
SMEM = pl.BlockSpec(memory_space=pltpu.SMEM)
ANY = pl.BlockSpec(memory_space=pl.ANY)


def passed_along(block, axis, distance):
    devices = range(lax.axis_size(axis))
    route = [((i - distance) % len(devices), i) for i in devices]
    return lax.ppermute(block, axis, route)


def swapped(block, axis):
    return lax.ppermute(block, axis, [(i, i ^ 1) for i in range(lax.axis_size(axis))])


def times_links(field_ref, coef_ref, roll, store):
    count, sites = field_ref.shape[1:]
    for t in range(sites // LANES):
        lanes = slice(t * LANES, (t + 1) * LANES)

        def coef(part, a, b):
            row = (part * 3 + a) * 3 + b
            return jnp.broadcast_to(coef_ref[row : row + 1, lanes], (ROWS, LANES))

        u = [[[coef(p, a, b) for b in range(3)] for a in range(3)] for p in range(2)]
        if roll:
            lane = lax.broadcasted_iota(jnp.int32, (ROWS, LANES), 1)
            last = (lane & (X - 1)) == X - 1

        def body(m, carry):
            rows = pl.ds(pl.multiple_of(m * ROWS, ROWS), ROWS)
            v = []
            for k in range(6):
                value = field_ref[k, rows, lanes].astype(jnp.float32)
                if roll:
                    ahead = pltpu.roll(value, LANES - 1, 1)
                    around = pltpu.roll(value, X - 1, 1)
                    value = jnp.where(last, around, ahead)
                v.append(value)
            re, im = v[:3], v[3:]
            for a in range(3):
                ur, ui = u[0][a], u[1][a]
                dr = ur[0] * re[0] - ui[0] * im[0]
                di = ur[0] * im[0] + ui[0] * re[0]
                for b in (1, 2):
                    dr = dr + (ur[b] * re[b] - ui[b] * im[b])
                    di = di + (ur[b] * im[b] + ui[b] * re[b])
                store(0, a, m, lanes, dr.astype(jnp.bfloat16))
                store(1, a, m, lanes, di.astype(jnp.bfloat16))
            return carry

        lax.fori_loop(0, count // ROWS, body, 0, unroll=2)


def rows_by_own(slabs, own):
    return slabs % 4 == 0 and own % 8 == 0


def inner(left, right):
    return lax.dot_general(left, right, (((1,), (1,)), ((), ())), preferred_element_type=jnp.float32)


def finish(sum_re, sum_im, slabs, core, order, acc, send, keep):
    count = send.shape[0]
    own = count // slabs
    acc[0] = sum_re - sum_re.T
    acc[1] = sum_im + sum_im.T
    if not rows_by_own(slabs, own):
        send[...] = acc[1 - core].astype(jnp.bfloat16)
        keep[...] = acc[core]
        return
    for k in range(slabs // 2):
        block = slice(k * 2 * own, (k + 1) * 2 * own)

        def rows(which):
            at = pl.ds(pl.multiple_of((2 * order[k] + which) * own, 8), own)
            return jnp.concatenate([acc[0, at, :], acc[1, at, :]], axis=0)

        send[block, :] = rows(1 - core).astype(jnp.bfloat16)
        keep[block, :] = rows(core)


def x_kernel(slabs, where_ref, field_ref, links_ref, send, keep, right, acc):
    count = field_ref.shape[1]

    def store(part, a, m, lanes, value):
        right[a, pl.ds(pl.multiple_of(part * count + m * ROWS, ROWS), ROWS), lanes] = value

    times_links(field_ref, links_ref, True, store)
    product = [None, None]
    for b in range(3):
        for part in range(2):
            term = inner(field_ref[part * 3 + b], right[b])
            product[part] = term if b == 0 else product[part] + term
    sum_re = product[0][:, :count] + product[1][:, count:]
    sum_im = product[0][:, count:] - product[1][:, :count]
    finish(sum_re, sum_im, slabs, where_ref[0], range(slabs // 2), acc, send, keep)


def cut_kernel(where_ref, field_ref, half_ref):
    half_ref[...] = field_ref[...]


def cut(where, field):
    parts, count, sites = field.shape
    block = (1, count, sites // 2)
    return pl.pallas_call(
        cut_kernel,
        out_shape=jax.ShapeDtypeStruct((parts, count, sites // 2), field.dtype),
        grid_spec=pltpu.PrefetchScalarGridSpec(
            num_scalar_prefetch=1,
            grid=(parts,),
            in_specs=[pl.BlockSpec(block, lambda k, where_ref: (k, 0, where_ref[0]))],
            out_specs=pl.BlockSpec(block, lambda k, where_ref: (k, 0, 0)),
        ),
        compiler_params=pltpu.CompilerParams(vmem_limit_bytes=60 * 2**20),
    )(where, field)


def b_kernel(field_ref, coef_ref, after_ref, b_ref):
    count, sites = field_ref.shape[1:]
    half = sites // 2

    def store(part, a, m, lanes, value):
        rows = pl.ds(pl.multiple_of(part * count + m * ROWS, ROWS), ROWS)
        start = a * half + lanes.start % half
        b_ref[lanes.start // half, rows, start : start + LANES] = value

    times_links(field_ref, coef_ref, False, store)


def z_order(chip, chips):
    along = chips // 2
    ahead = [lax.rem((chip >> 1) + r, along) * 2 for r in range(along)]
    low = chip & 1
    return [to + 1 - low for to in ahead] + [to + low for to in ahead]


def z_kernel(near, slabs, where_ref, b_ref, got_hbm, *refs):
    if near:
        out, right, sems = refs
    else:
        before, send, keep, right, acc, sems = refs
    count, half = got_hbm.shape[1], right.shape[1] // 3
    core = where_ref[0]
    which = core if near else 1 - core
    lanes = pl.ds(pl.multiple_of(which * half, LANES), half) if near else pl.ds(0, half)
    copies = []
    for part in range(2):
        for b in range(3):
            k = part * 3 + b
            to = right.at[pl.ds(part * count, count), pl.ds(b * half, half)]
            copies.append(pltpu.make_async_copy(got_hbm.at[k, :, lanes], to, sems.at[k]))
    for copy in copies:
        copy.start()
    for copy in copies:
        copy.wait()
    sign = (1 - 2 * which).astype(jnp.float32)
    from_re = inner(b_ref[which, :count, :], right[...])
    from_im = inner(b_ref[which, count:, :], right[...])
    sum_re = (from_re[:, :count] + from_im[:, count:]) * sign
    sum_im = (from_re[:, count:] - from_im[:, :count]) * sign
    if near:
        out[0] = sum_re
        out[1] = sum_im
    else:
        order = z_order(where_ref[1], slabs // 2)
        finish(before[0] + sum_re, before[1] + sum_im, slabs, core, order, acc, send, keep)


def call(body, outs, specs, scratch, mib, flops, moved):
    return pl.pallas_call(
        body,
        out_shape=outs,
        in_specs=specs,
        out_specs=[VMEM] * len(outs),
        scratch_shapes=scratch,
        compiler_params=pltpu.CompilerParams(vmem_limit_bytes=mib * 2**20),
        cost_estimate=pl.CostEstimate(flops=flops, bytes_accessed=moved, transcendentals=0),
    )


def shards(vectors, links):
    slabs = lax.axis_size("gz")
    count, planes, sites = vectors.shape[1], vectors.shape[3], vectors.shape[4]
    assert planes == 1 and slabs % 2 == 0
    own = count // slabs
    scale = 1.0 / math.sqrt(12.0 * sites * planes * slabs)
    index = lax.axis_index("gz").astype(jnp.int32)
    where = jnp.stack([index & 1, index >> 1])
    field = jnp.transpose(vectors, (0, 2, 3, 1, 4)).reshape(6, count, sites)
    half = sites // 2
    piece = cut(where, field)
    far = lax.ppermute(piece, "gz", [(i, (i + i % 2 * 2 - 1) % slabs) for i in range(slabs)])
    links = links.reshape(2, 2, 3, 3, sites)
    links_x, links_z = links[:, 0].reshape(18, sites), links[:, 1]
    whole, links_x = lax.optimization_barrier((field, links_x))
    near = swapped(whole, "gz")
    conjugate = jnp.array([1.0, -1.0], jnp.float32).reshape(2, 1, 1, 1)
    adjoint = jnp.transpose(links_z[..., :half], (0, 2, 1, 3)) * conjugate
    coefs = jnp.concatenate([adjoint, passed_along(links_z[..., half:], "gz", 1)], axis=-1)
    coefs = coefs.reshape(18, sites)

    flops = 24 * count * count * sites
    moved = 12 * count * sites
    halves = [
        jax.ShapeDtypeStruct((count, count), jnp.bfloat16),
        jax.ShapeDtypeStruct((count, count), jnp.float32),
    ]
    stacked = pltpu.VMEM((3, 2 * count, sites), jnp.bfloat16)
    square = pltpu.VMEM((2, count, count), jnp.float32)
    send_x, keep_x = call(
        functools.partial(x_kernel, slabs), halves, [SMEM, VMEM, VMEM],
        [stacked, square], 16, flops, moved,
    )(where, field, links_x)
    chip_x = (keep_x + swapped(send_x, "gz").astype(jnp.float32)).astype(jnp.bfloat16)
    (prepared,) = call(
        b_kernel, [jax.ShapeDtypeStruct((2, 2 * count, 3 * half), jnp.bfloat16)], [VMEM, VMEM, ANY],
        [], 10, count * sites * 66, 2 * moved,
    )(field, coefs, chip_x)
    right = [pltpu.VMEM((2 * count, 3 * half), jnp.bfloat16)]
    sems = [pltpu.SemaphoreType.DMA((6,))]
    (first,) = call(
        functools.partial(z_kernel, True, slabs), [jax.ShapeDtypeStruct((2, count, count), jnp.float32)],
        [SMEM, VMEM, ANY], right + sems, 14, flops // 2, moved // 2,
    )(where, prepared, near)

    if rows_by_own(slabs, own):
        groups = [list(range(c, slabs, 2)) for c in range(2)]
        blocks = (slabs // 2, 1, 2 * own, count)
    else:
        groups = None
        blocks = (slabs // 2, 2, own, count)

    def exchanged(chip):
        chip = chip.reshape((-1,) + blocks[2:])
        return lax.all_to_all(chip, "gz", 0, 0, axis_index_groups=groups)

    def total(got):
        return jnp.sum(got.reshape(blocks).astype(jnp.float32), axis=0).reshape(2, own, count)

    got_x = exchanged(chip_x)
    send_z, keep_z = call(
        functools.partial(z_kernel, False, slabs), halves, [SMEM, VMEM, ANY, VMEM],
        right + [square] + sems, 14, flops // 2, moved // 2,
    )(where, prepared, far, first)
    send_z, got_x = lax.optimization_barrier((send_z, got_x))
    chip_z = keep_z + swapped(send_z, "gz").astype(jnp.float32)
    if rows_by_own(slabs, own):
        rows = count // 2
        other = chip_z[:rows].astype(jnp.bfloat16)
        near = lax.ppermute(other, "gz", [(i, i ^ 2) for i in range(slabs)])
        line = chip_z[rows:] + near.astype(jnp.float32)
        total_z = line[: 2 * own]
        for r in range(1, slabs // 4):
            block = line[r * 2 * own : (r + 1) * 2 * own].astype(jnp.bfloat16)
            total_z = total_z + passed_along(block, "gz", 4 * r).astype(jnp.float32)
        total_z = total_z.reshape(2, own, count)
    else:
        total_z = total(exchanged(chip_z.astype(jnp.bfloat16)))
    both = jnp.concatenate([total(got_x), total_z], axis=0)
    return jnp.transpose(both, (1, 0, 2)) * scale


def solution(mesh):
    return jax.shard_map(
        shards,
        mesh=mesh,
        in_specs=(P("grp", None, None, "gz", None), P("grp", None, None, None, "gz", None)),
        out_specs=P("gz", "grp", None),
        check_vma=False,
    )
```

```python
import functools
import math

import jax
import jax.numpy as jnp
from jax import lax
from jax.experimental import pallas as pl
from jax.experimental.pallas import tpu as pltpu
from jax.sharding import PartitionSpec as P

X = 64
LANES = 128
ROWS = 16
VMEM = pl.BlockSpec(memory_space=pltpu.VMEM)
SMEM = pl.BlockSpec(memory_space=pltpu.SMEM)
ANY = pl.BlockSpec(memory_space=pl.ANY)


def passed_along(block, axis, distance):
    devices = range(lax.axis_size(axis))
    route = [((i - distance) % len(devices), i) for i in devices]
    return lax.ppermute(block, axis, route)


def swapped(block, axis):
    return lax.ppermute(block, axis, [(i, i ^ 1) for i in range(lax.axis_size(axis))])


def times_links(field_ref, links_ref, mu, adjoint, roll, store):
    count, sites = field_ref.shape[1:]
    for t in range(sites // LANES):
        lanes = slice(t * LANES, (t + 1) * LANES)

        def link(part, a, b):
            row = ((part * 2 + mu) * 3 + a) * 3 + b
            value = jnp.broadcast_to(links_ref[row : row + 1, lanes], (ROWS, LANES))
            return -value if adjoint and part == 1 else value

        def links_of(part, a):
            return [link(part, b, a) if adjoint else link(part, a, b) for b in range(3)]

        u = [[links_of(p, a) for a in range(3)] for p in range(2)]
        if roll:
            lane = lax.broadcasted_iota(jnp.int32, (ROWS, LANES), 1)
            last = (lane & (X - 1)) == X - 1

        def body(m, carry):
            rows = pl.ds(pl.multiple_of(m * ROWS, ROWS), ROWS)
            v = []
            for k in range(6):
                value = field_ref[k, rows, lanes].astype(jnp.float32)
                if roll:
                    ahead = pltpu.roll(value, LANES - 1, 1)
                    around = pltpu.roll(value, X - 1, 1)
                    value = jnp.where(last, around, ahead)
                v.append(value)
            re, im = v[:3], v[3:]
            for a in range(3):
                ur, ui = u[0][a], u[1][a]
                dr = ur[0] * re[0] - ui[0] * im[0]
                di = ur[0] * im[0] + ui[0] * re[0]
                for b in (1, 2):
                    dr = dr + (ur[b] * re[b] - ui[b] * im[b])
                    di = di + (ur[b] * im[b] + ui[b] * re[b])
                store(0, a, m, lanes, dr.astype(jnp.bfloat16))
                store(1, a, m, lanes, di.astype(jnp.bfloat16))
            return carry

        lax.fori_loop(0, count // ROWS, body, 0, unroll=2)


def rows_by_own(slabs, own):
    return slabs % 4 == 0 and own % 8 == 0


def inner(left, right):
    return lax.dot_general(left, right, (((1,), (1,)), ((), ())), preferred_element_type=jnp.float32)


def block_order(chip, chips):
    along = chips // 2
    ahead = [lax.rem((chip >> 1) + r, along) * 2 for r in range(along)]
    low = chip & 1
    return [to + 1 - low for to in ahead] + [to + low for to in ahead]


def finish(sum_re, sum_im, slabs, chip, acc, store):
    count = acc.shape[1]
    own = count // slabs
    acc[0] = sum_re - sum_re.T
    acc[1] = sum_im + sum_im.T
    if not rows_by_own(slabs, own):
        for k in range(2):
            store(k, acc[k])
        return
    for k, to in enumerate(block_order(chip, slabs // 2)):
        rows = [pl.ds(pl.multiple_of((2 * to + core) * own, 8), own) for core in range(2)]
        store(k, jnp.concatenate([acc[part, at, :] for at in rows for part in range(2)], axis=0))


def x_kernel(slabs, where_ref, field_ref, links_ref, send, keep, right, acc):
    count = field_ref.shape[1]

    def store(part, a, m, lanes, value):
        right[a, pl.ds(pl.multiple_of(part * count + m * ROWS, ROWS), ROWS), lanes] = value

    times_links(field_ref, links_ref, 0, False, True, store)
    product = [None, None]
    for b in range(3):
        for part in range(2):
            term = inner(field_ref[part * 3 + b], right[b])
            product[part] = term if b == 0 else product[part] + term
    sum_re = product[0][:, :count] + product[1][:, count:]
    sum_im = product[0][:, count:] - product[1][:, :count]

    def store(k, rows):
        size = rows.shape[0]
        send[k * size : (k + 1) * size, :] = rows.astype(jnp.bfloat16)
        keep[k * size : (k + 1) * size, :] = rows

    finish(sum_re, sum_im, slabs, where_ref[1], acc, store)


def w_kernel(field_ref, links_ref, w_ref):
    def store(part, a, m, lanes, value):
        w_ref[part * 3 + a, pl.ds(pl.multiple_of(m * ROWS, ROWS), ROWS), lanes] = value

    times_links(field_ref, links_ref, 1, True, False, store)


def z_kernel(far, slabs, where_ref, w_ref, face_hbm, *refs):
    if far:
        before, other, mine, right, acc, sems = refs
    else:
        out, right, acc, sems = refs
    count = w_ref.shape[1]
    copies = []
    for b in range(3):
        group = []
        for part in range(2):
            k = part * 3 + b
            rows = pl.ds(part * count, count)
            group.append(pltpu.make_async_copy(face_hbm.at[k], right.at[b, rows], sems.at[k]))
        for copy in group:
            copy.start()
        copies.append(group)
    product = [None, None]
    for b in range(3):
        for copy in copies[b]:
            copy.wait()
        for part in range(2):
            term = inner(w_ref[part * 3 + b], right[b])
            product[part] = term if b == 0 else product[part] + term
    sum_re = product[0][:, :count] + product[1][:, count:]
    sum_im = product[0][:, count:] - product[1][:, :count]

    def store(k, rows):
        size = rows.shape[0]
        at = slice(k * size, (k + 1) * size)
        if not far:
            out[at, :] = rows.astype(jnp.bfloat16)
            return
        rows = rows + before[at, :].astype(jnp.float32)
        if at.start < count:
            other[at, :] = rows.astype(jnp.bfloat16)
        else:
            mine[at.start - count : at.stop - count, :] = rows

    finish(sum_re, sum_im, slabs, where_ref[1], acc, store)


def call(body, outs, specs, scratch, mib, flops, moved):
    return pl.pallas_call(
        body,
        out_shape=outs,
        in_specs=specs,
        out_specs=[VMEM] * len(outs),
        scratch_shapes=scratch,
        compiler_params=pltpu.CompilerParams(vmem_limit_bytes=mib * 2**20),
        cost_estimate=pl.CostEstimate(flops=flops, bytes_accessed=moved, transcendentals=0),
    )


def shards(vectors, links):
    slabs = lax.axis_size("gz")
    count, planes, sites = vectors.shape[1], vectors.shape[3], vectors.shape[4]
    assert planes == 1 and slabs % 2 == 0
    own = count // slabs
    scale = 1.0 / math.sqrt(12.0 * sites * planes * slabs)
    index = lax.axis_index("gz").astype(jnp.int32)
    where = jnp.stack([index & 1, index >> 1])
    field = jnp.transpose(vectors, (0, 2, 3, 1, 4)).reshape(6, count, sites)
    links = links.reshape(36, sites)
    far = lax.ppermute(field, "gz", [(i, (i - 1) % slabs) for i in range(0, slabs, 2)])
    near = lax.ppermute(field, "gz", [(i, i - 1) for i in range(1, slabs, 2)])

    flops = 24 * count * count * sites
    moved = 12 * count * sites
    halves = [
        jax.ShapeDtypeStruct((count, count), jnp.bfloat16),
        jax.ShapeDtypeStruct((count, count), jnp.float32),
    ]
    whole = [jax.ShapeDtypeStruct((2 * count, count), half.dtype) for half in halves]
    stacked = pltpu.VMEM((3, 2 * count, sites), jnp.bfloat16)
    square = pltpu.VMEM((2, count, count), jnp.float32)
    send_x, keep_x = call(
        functools.partial(x_kernel, slabs), whole, [SMEM, VMEM, VMEM],
        [stacked, square], 18, flops, moved,
    )(where, field, links)
    (w,) = call(
        w_kernel, [jax.ShapeDtypeStruct(field.shape, jnp.bfloat16)], [VMEM, VMEM], [], 10,
        count * sites * 66, 2 * moved,
    )(field, links)
    scratch = [stacked, square, pltpu.SemaphoreType.DMA((6,))]
    (early,) = call(
        functools.partial(z_kernel, False, slabs), whole[:1], [SMEM, VMEM, ANY],
        scratch, 16, flops, moved,
    )(where, w, near)

    def late(before):
        return call(
            functools.partial(z_kernel, True, slabs), halves, [SMEM, VMEM, ANY, VMEM],
            scratch, 16, flops, moved,
        )(where, w, far, before)

    if not rows_by_own(slabs, own):

        def exchanged(terms):
            terms = terms.astype(jnp.bfloat16).reshape(2, slabs, own, count)
            got = lax.all_to_all(jnp.transpose(terms, (1, 0, 2, 3)), "gz", 0, 0)
            return jnp.sum(got.astype(jnp.float32), axis=0)

        both = [exchanged(keep_x), exchanged(jnp.concatenate(late(early), axis=0))]
        return jnp.transpose(jnp.concatenate(both, axis=0), (1, 0, 2)) * scale

    def summed(other, mine, core):
        members = range(core, slabs, 2)

        def shifted(block, route):
            return lax.ppermute(block, "gz", [(i, route(i) % slabs) for i in members]).astype(jnp.float32)

        line = mine + shifted(other, lambda i: i ^ 2)
        result = line[: 4 * own]
        for r in range(1, slabs // 4):
            block = line[r * 4 * own : (r + 1) * 4 * own].astype(jnp.bfloat16)
            result = result + shifted(block, lambda i: i + 4 * r)
        return result

    got = lax.ppermute(send_x, "gz", [(i, i - 1) for i in range(1, slabs, 2)])
    chip_x = keep_x + got.astype(jnp.float32)
    sum_x = summed(chip_x[:count].astype(jnp.bfloat16), chip_x[count:], 0)
    before = lax.ppermute(early, "gz", [(i, i + 1) for i in range(0, slabs, 2)])
    sum_z = summed(*late(before), 1)
    even = where[0] == 0
    here, there = slice(0, 2 * own), slice(2 * own, 4 * own)
    got = swapped(jnp.where(even, sum_x[there], sum_z[here]), "gz")
    both = [jnp.where(even, sum_x[here], got), jnp.where(even, got, sum_z[there])]
    both = jnp.concatenate(both, axis=0).reshape(4, own, count)
    return jnp.transpose(both, (1, 0, 2)) * scale


def solution(mesh):
    return jax.shard_map(
        shards,
        mesh=mesh,
        in_specs=(P("grp", None, None, "gz", None), P("grp", None, None, None, "gz", None)),
        out_specs=P("gz", "grp", None),
        check_vma=False,
    )
```

```python
import functools
import math

import jax
import jax.numpy as jnp
from jax import lax
from jax.experimental import pallas as pl
from jax.experimental.pallas import tpu as pltpu
from jax.sharding import PartitionSpec as P

X = 64
LANES = 128
ROWS = 16
VMEM = pl.BlockSpec(memory_space=pltpu.VMEM)
SMEM = pl.BlockSpec(memory_space=pltpu.SMEM)
ANY = pl.BlockSpec(memory_space=pl.ANY)


def passed_along(block, axis, distance):
    devices = range(lax.axis_size(axis))
    route = [((i - distance) % len(devices), i) for i in devices]
    return lax.ppermute(block, axis, route)


def swapped(block, axis):
    return lax.ppermute(block, axis, [(i, i ^ 1) for i in range(lax.axis_size(axis))])


def times_links(field_ref, links_ref, mu, adjoint, roll, store):
    count, sites = field_ref.shape[1:]
    for t in range(sites // LANES):
        lanes = slice(t * LANES, (t + 1) * LANES)

        def link(part, a, b):
            row = ((part * 2 + mu) * 3 + a) * 3 + b
            value = jnp.broadcast_to(links_ref[row : row + 1, lanes], (ROWS, LANES))
            return -value if adjoint and part == 1 else value

        def links_of(part, a):
            return [link(part, b, a) if adjoint else link(part, a, b) for b in range(3)]

        u = [[links_of(p, a) for a in range(3)] for p in range(2)]
        if roll:
            lane = lax.broadcasted_iota(jnp.int32, (ROWS, LANES), 1)
            last = (lane & (X - 1)) == X - 1

        def body(m, carry):
            rows = pl.ds(pl.multiple_of(m * ROWS, ROWS), ROWS)
            v = []
            for k in range(6):
                value = field_ref[k, rows, lanes].astype(jnp.float32)
                if roll:
                    ahead = pltpu.roll(value, LANES - 1, 1)
                    around = pltpu.roll(value, X - 1, 1)
                    value = jnp.where(last, around, ahead)
                v.append(value)
            re, im = v[:3], v[3:]
            for a in range(3):
                ur, ui = u[0][a], u[1][a]
                dr = ur[0] * re[0] - ui[0] * im[0]
                di = ur[0] * im[0] + ui[0] * re[0]
                for b in (1, 2):
                    dr = dr + (ur[b] * re[b] - ui[b] * im[b])
                    di = di + (ur[b] * im[b] + ui[b] * re[b])
                store(0, a, m, lanes, dr.astype(jnp.bfloat16))
                store(1, a, m, lanes, di.astype(jnp.bfloat16))
            return carry

        lax.fori_loop(0, count // ROWS, body, 0, unroll=2)


def rows_by_own(slabs, own):
    return slabs % 4 == 0 and own % 8 == 0


def inner(left, right):
    return lax.dot_general(left, right, (((1,), (1,)), ((), ())), preferred_element_type=jnp.float32)


def finish(sum_re, sum_im, slabs, core, order, acc, sends, keeps):
    count = acc.shape[1]
    own = count // slabs
    acc[0] = sum_re - sum_re.T
    acc[1] = sum_im + sum_im.T
    if not rows_by_own(slabs, own):
        size = count // 2
        for piece in range(len(sends)):
            at = slice(piece * size, (piece + 1) * size) if len(sends) == 2 else slice(0, count)
            sends[piece][...] = acc[1 - core, at, :].astype(jnp.bfloat16)
            keeps[piece][...] = acc[core, at, :]
        return
    each = len(order) // len(sends)
    for k, to in enumerate(order):
        block = slice(k % each * 2 * own, (k % each + 1) * 2 * own)

        def rows(which):
            at = pl.ds(pl.multiple_of((2 * to + which) * own, 8), own)
            return jnp.concatenate([acc[0, at, :], acc[1, at, :]], axis=0)

        sends[k // each][block, :] = rows(1 - core).astype(jnp.bfloat16)
        keeps[k // each][block, :] = rows(core)


def x_kernel(slabs, where_ref, field_ref, links_ref, send, keep, right, acc):
    count = field_ref.shape[1]

    def store(part, a, m, lanes, value):
        right[a, pl.ds(pl.multiple_of(part * count + m * ROWS, ROWS), ROWS), lanes] = value

    times_links(field_ref, links_ref, 0, False, True, store)
    product = [None, None]
    for b in range(3):
        for part in range(2):
            term = inner(field_ref[part * 3 + b], right[b])
            product[part] = term if b == 0 else product[part] + term
    sum_re = product[0][:, :count] + product[1][:, count:]
    sum_im = product[0][:, count:] - product[1][:, :count]
    finish(sum_re, sum_im, slabs, where_ref[0], range(slabs // 2), acc, [send], [keep])


def w_kernel(field_ref, links_ref, after_ref, w_ref):
    def store(part, a, m, lanes, value):
        w_ref[part * 3 + a, pl.ds(pl.multiple_of(m * ROWS, ROWS), ROWS), lanes] = value

    times_links(field_ref, links_ref, 1, True, False, store)


def z_order(chip, chips):
    along = chips // 2
    ahead = [lax.rem((chip >> 1) + r, along) * 2 for r in range(along)]
    low = chip & 1
    return [to + 1 - low for to in ahead] + [to + low for to in ahead]


def z_kernel(slabs, where_ref, w_ref, face_hbm, *refs):
    sends, keeps, (right, acc, sems) = refs[:2], refs[2:4], refs[4:]
    count = w_ref.shape[1]
    copies = []
    for b in range(3):
        group = []
        for part in range(2):
            k = part * 3 + b
            rows = pl.ds(part * count, count)
            group.append(pltpu.make_async_copy(face_hbm.at[k], right.at[b, rows], sems.at[k]))
        for copy in group:
            copy.start()
        copies.append(group)
    product = [None, None]
    for b in range(3):
        for copy in copies[b]:
            copy.wait()
        for part in range(2):
            term = inner(w_ref[part * 3 + b], right[b])
            product[part] = term if b == 0 else product[part] + term
    sum_re = product[0][:, :count] + product[1][:, count:]
    sum_im = product[0][:, count:] - product[1][:, :count]
    finish(sum_re, sum_im, slabs, where_ref[0], z_order(where_ref[1], slabs // 2), acc, sends, keeps)


def call(body, outs, specs, scratch, mib, flops, moved):
    return pl.pallas_call(
        body,
        out_shape=outs,
        in_specs=specs,
        out_specs=[VMEM] * len(outs),
        scratch_shapes=scratch,
        compiler_params=pltpu.CompilerParams(vmem_limit_bytes=mib * 2**20),
        cost_estimate=pl.CostEstimate(flops=flops, bytes_accessed=moved, transcendentals=0),
    )


def shards(vectors, links):
    slabs = lax.axis_size("gz")
    count, planes, sites = vectors.shape[1], vectors.shape[3], vectors.shape[4]
    assert planes == 1 and slabs % 2 == 0
    own = count // slabs
    scale = 1.0 / math.sqrt(12.0 * sites * planes * slabs)
    index = lax.axis_index("gz").astype(jnp.int32)
    where = jnp.stack([index & 1, index >> 1])
    field = jnp.transpose(vectors, (0, 2, 3, 1, 4)).reshape(6, count, sites)
    links = links.reshape(36, sites)
    face = passed_along(field, "gz", -1)

    flops = 24 * count * count * sites
    moved = 12 * count * sites
    halves = [
        jax.ShapeDtypeStruct((count, count), jnp.bfloat16),
        jax.ShapeDtypeStruct((count, count), jnp.float32),
    ]
    stacked = pltpu.VMEM((3, 2 * count, sites), jnp.bfloat16)
    square = pltpu.VMEM((2, count, count), jnp.float32)
    send_x, keep_x = call(
        functools.partial(x_kernel, slabs), halves, [SMEM, VMEM, VMEM],
        [stacked, square], 16, flops, moved,
    )(where, field, links)
    chip_x = (keep_x + swapped(send_x, "gz").astype(jnp.float32)).astype(jnp.bfloat16)
    (w,) = call(
        w_kernel, [jax.ShapeDtypeStruct(field.shape, jnp.bfloat16)], [VMEM, VMEM, ANY], [], 10,
        count * sites * 66, 2 * moved,
    )(field, links, chip_x)

    if rows_by_own(slabs, own):
        groups = [list(range(c, slabs, 2)) for c in range(2)]
        blocks = (slabs // 2, 1, 2 * own, count)
    else:
        groups = None
        blocks = (slabs // 2, 2, own, count)

    def exchanged(chip):
        chip = chip.reshape((-1,) + blocks[2:])
        return lax.all_to_all(chip, "gz", 0, 0, axis_index_groups=groups)

    def total(got):
        return jnp.sum(got.reshape(blocks).astype(jnp.float32), axis=0).reshape(2, own, count)

    got_x = exchanged(chip_x)
    quarters = [jax.ShapeDtypeStruct((count // 2, count), h.dtype) for h in halves for _ in range(2)]
    send_other, send_mine, keep_other, keep_mine = call(
        functools.partial(z_kernel, slabs), quarters, [SMEM, VMEM, ANY],
        [stacked, square, pltpu.SemaphoreType.DMA((6,))], 14, flops, moved,
    )(where, w, face)
    send_other, got_x = lax.optimization_barrier((send_other, got_x))
    other = keep_other + swapped(send_other, "gz").astype(jnp.float32)
    mine = keep_mine + swapped(send_mine, "gz").astype(jnp.float32)
    if rows_by_own(slabs, own):
        along = slabs // 4
        size = 2 * own
        near = lax.ppermute(other.astype(jnp.bfloat16), "gz", [(i, i ^ 2) for i in range(slabs)])
        line = mine + near.astype(jnp.float32)
        total_z = line[:size]
        for r in range(1, along):
            block = line[r * size : (r + 1) * size].astype(jnp.bfloat16)
            total_z = total_z + passed_along(block, "gz", 4 * r).astype(jnp.float32)
        total_z = total_z.reshape(2, own, count)
    else:
        chip_z = jnp.concatenate([other, mine], axis=0)
        total_z = total(exchanged(chip_z.astype(jnp.bfloat16)))
    both = jnp.concatenate([total(got_x), total_z], axis=0)
    return jnp.transpose(both, (1, 0, 2)) * scale


def solution(mesh):
    return jax.shard_map(
        shards,
        mesh=mesh,
        in_specs=(P("grp", None, None, "gz", None), P("grp", None, None, None, "gz", None)),
        out_specs=P("gz", "grp", None),
        check_vma=False,
    )
```

```python
import functools
import math

import jax
import jax.numpy as jnp
from jax import lax
from jax.experimental import pallas as pl
from jax.experimental.pallas import tpu as pltpu
from jax.sharding import PartitionSpec as P

X = 64
LANES = 128
ROWS = 16
VMEM = pl.BlockSpec(memory_space=pltpu.VMEM)
SMEM = pl.BlockSpec(memory_space=pltpu.SMEM)
ANY = pl.BlockSpec(memory_space=pl.ANY)


def passed_along(block, axis, distance):
    devices = range(lax.axis_size(axis))
    route = [((i - distance) % len(devices), i) for i in devices]
    return lax.ppermute(block, axis, route)


def swapped(block, axis):
    return lax.ppermute(block, axis, [(i, i ^ 1) for i in range(lax.axis_size(axis))])


def times_links(field_ref, links_ref, mu, adjoint, roll, store):
    count, sites = field_ref.shape[1:]
    for t in range(sites // LANES):
        lanes = slice(t * LANES, (t + 1) * LANES)

        def link(part, a, b):
            row = ((part * 2 + mu) * 3 + a) * 3 + b
            value = jnp.broadcast_to(links_ref[row : row + 1, lanes], (ROWS, LANES))
            return -value if adjoint and part == 1 else value

        def links_of(part, a):
            return [link(part, b, a) if adjoint else link(part, a, b) for b in range(3)]

        u = [[links_of(p, a) for a in range(3)] for p in range(2)]
        if roll:
            lane = lax.broadcasted_iota(jnp.int32, (ROWS, LANES), 1)
            last = (lane & (X - 1)) == X - 1

        def body(m, carry):
            rows = pl.ds(pl.multiple_of(m * ROWS, ROWS), ROWS)
            v = []
            for k in range(6):
                value = field_ref[k, rows, lanes].astype(jnp.float32)
                if roll:
                    ahead = pltpu.roll(value, LANES - 1, 1)
                    around = pltpu.roll(value, X - 1, 1)
                    value = jnp.where(last, around, ahead)
                v.append(value)
            re, im = v[:3], v[3:]
            for a in range(3):
                ur, ui = u[0][a], u[1][a]
                dr = ur[0] * re[0] - ui[0] * im[0]
                di = ur[0] * im[0] + ui[0] * re[0]
                for b in (1, 2):
                    dr = dr + (ur[b] * re[b] - ui[b] * im[b])
                    di = di + (ur[b] * im[b] + ui[b] * re[b])
                store(0, a, m, lanes, dr.astype(jnp.bfloat16))
                store(1, a, m, lanes, di.astype(jnp.bfloat16))
            return carry

        lax.fori_loop(0, count // ROWS, body, 0, unroll=2)


def rows_by_own(slabs, own):
    return slabs % 4 == 0 and own % 8 == 0 and slabs & (slabs - 1) == 0


def inner(left, right):
    return lax.dot_general(left, right, (((1,), (1,)), ((), ())), preferred_element_type=jnp.float32)


def finish(sum_re, sum_im, slabs, core, order, acc, send, keep):
    count = send.shape[0]
    own = count // slabs
    acc[0] = sum_re - sum_re.T
    acc[1] = sum_im + sum_im.T
    if not rows_by_own(slabs, own):
        send[...] = acc[1 - core].astype(jnp.bfloat16)
        keep[...] = acc[core]
        return
    for k in range(slabs // 2):
        block = slice(k * 2 * own, (k + 1) * 2 * own)

        def rows(which):
            at = pl.ds(pl.multiple_of((2 * order[k] + which) * own, 8), own)
            return jnp.concatenate([acc[0, at, :], acc[1, at, :]], axis=0)

        send[block, :] = rows(1 - core).astype(jnp.bfloat16)
        keep[block, :] = rows(core)


def x_kernel(slabs, where_ref, field_ref, links_ref, send, keep, right, acc):
    count = field_ref.shape[1]

    def store(part, a, m, lanes, value):
        right[a, pl.ds(pl.multiple_of(part * count + m * ROWS, ROWS), ROWS), lanes] = value

    times_links(field_ref, links_ref, 0, False, True, store)
    product = [None, None]
    for b in range(3):
        for part in range(2):
            term = inner(field_ref[part * 3 + b], right[b])
            product[part] = term if b == 0 else product[part] + term
    sum_re = product[0][:, :count] + product[1][:, count:]
    sum_im = product[0][:, count:] - product[1][:, :count]
    finish(sum_re, sum_im, slabs, where_ref[0], range(slabs // 2), acc, send, keep)


def w_kernel(field_ref, links_ref, after_ref, w_ref):
    def store(part, a, m, lanes, value):
        w_ref[part * 3 + a, pl.ds(pl.multiple_of(m * ROWS, ROWS), ROWS), lanes] = value

    times_links(field_ref, links_ref, 1, True, False, store)


def z_order(chip, chips):
    flips = [0]
    for bit in reversed(range(chips.bit_length() - 1)):
        flips = [flip | 1 << bit for flip in flips] + flips
    return [chip ^ flip for flip in flips]


def z_kernel(slabs, where_ref, w_ref, face_hbm, send, keep, right, acc, sems):
    count = w_ref.shape[1]
    copies = []
    for b in range(3):
        group = []
        for part in range(2):
            k = part * 3 + b
            rows = pl.ds(part * count, count)
            group.append(pltpu.make_async_copy(face_hbm.at[k], right.at[b, rows], sems.at[k]))
        for copy in group:
            copy.start()
        copies.append(group)
    product = [None, None]
    for b in range(3):
        for copy in copies[b]:
            copy.wait()
        for part in range(2):
            term = inner(w_ref[part * 3 + b], right[b])
            product[part] = term if b == 0 else product[part] + term
    sum_re = product[0][:, :count] + product[1][:, count:]
    sum_im = product[0][:, count:] - product[1][:, :count]
    finish(sum_re, sum_im, slabs, where_ref[0], z_order(where_ref[1], slabs // 2), acc, send, keep)


def call(body, outs, specs, scratch, mib, flops, moved):
    return pl.pallas_call(
        body,
        out_shape=outs,
        in_specs=specs,
        out_specs=[VMEM] * len(outs),
        scratch_shapes=scratch,
        compiler_params=pltpu.CompilerParams(vmem_limit_bytes=mib * 2**20),
        cost_estimate=pl.CostEstimate(flops=flops, bytes_accessed=moved, transcendentals=0),
    )


def shards(vectors, links):
    slabs = lax.axis_size("gz")
    count, planes, sites = vectors.shape[1], vectors.shape[3], vectors.shape[4]
    assert planes == 1 and slabs % 2 == 0
    own = count // slabs
    scale = 1.0 / math.sqrt(12.0 * sites * planes * slabs)
    index = lax.axis_index("gz").astype(jnp.int32)
    where = jnp.stack([index & 1, index >> 1])
    field = jnp.transpose(vectors, (0, 2, 3, 1, 4)).reshape(6, count, sites)
    links = links.reshape(36, sites)
    face = passed_along(field, "gz", -1)

    flops = 24 * count * count * sites
    moved = 12 * count * sites
    halves = [
        jax.ShapeDtypeStruct((count, count), jnp.bfloat16),
        jax.ShapeDtypeStruct((count, count), jnp.float32),
    ]
    stacked = pltpu.VMEM((3, 2 * count, sites), jnp.bfloat16)
    square = pltpu.VMEM((2, count, count), jnp.float32)
    send_x, keep_x = call(
        functools.partial(x_kernel, slabs), halves, [SMEM, VMEM, VMEM],
        [stacked, square], 16, flops, moved,
    )(where, field, links)
    chip_x = (keep_x + swapped(send_x, "gz").astype(jnp.float32)).astype(jnp.bfloat16)
    (w,) = call(
        w_kernel, [jax.ShapeDtypeStruct(field.shape, jnp.bfloat16)], [VMEM, VMEM, ANY], [], 10,
        count * sites * 66, 2 * moved,
    )(field, links, chip_x)

    if rows_by_own(slabs, own):
        groups = [list(range(c, slabs, 2)) for c in range(2)]
        blocks = (slabs // 2, 1, 2 * own, count)
    else:
        groups = None
        blocks = (slabs // 2, 2, own, count)

    def exchanged(chip):
        chip = chip.reshape((-1,) + blocks[2:])
        return lax.all_to_all(chip, "gz", 0, 0, axis_index_groups=groups)

    def total(got):
        return jnp.sum(got.reshape(blocks).astype(jnp.float32), axis=0).reshape(2, own, count)

    got_x = exchanged(chip_x)
    send_z, keep_z = call(
        functools.partial(z_kernel, slabs), halves, [SMEM, VMEM, ANY],
        [stacked, square, pltpu.SemaphoreType.DMA((6,))], 14, flops, moved,
    )(where, w, face)
    send_z, got_x = lax.optimization_barrier((send_z, got_x))
    chip_z = keep_z + swapped(send_z, "gz").astype(jnp.float32)
    if rows_by_own(slabs, own):
        total_z = chip_z
        for bit in range(1, slabs.bit_length() - 1):
            half = total_z.shape[0] // 2
            route = [(i, i ^ (1 << bit)) for i in range(slabs)]
            got = lax.ppermute(total_z[:half].astype(jnp.bfloat16), "gz", route)
            total_z = total_z[half:] + got.astype(jnp.float32)
        total_z = total_z.reshape(2, own, count)
    else:
        total_z = total(exchanged(chip_z.astype(jnp.bfloat16)))
    both = jnp.concatenate([total(got_x), total_z], axis=0)
    return jnp.transpose(both, (1, 0, 2)) * scale


def solution(mesh):
    return jax.shard_map(
        shards,
        mesh=mesh,
        in_specs=(P("grp", None, None, "gz", None), P("grp", None, None, None, "gz", None)),
        out_specs=P("gz", "grp", None),
        check_vma=False,
    )
```
